32 devices in a mesh: span: 4 (over y, x), wall: 8 (over z, core).
Axes of the slice: x: 2, y: 2, z: 4, core: 2. Of those that a mesh axis runs over, the one named last changes fastest.
Arguments:
- forcing: bfloat16 [2, 5, 4, 128, 32, 128], P(None, None, None, 'span', 'wall'), may hold values from -6 to 6
- span_factor: float32 [2, 5, 128], replicated, may hold values from -1 to 1
- pivot_inverse: bfloat16 [2, 5, 5, 128, 32, 128], P(None, None, None, 'span', 'wall'), may hold values from -0.1875 to 0.1875
- step_lower: bfloat16 [2, 5, 5, 128, 32, 128], P(None, None, None, 'span', 'wall'), may hold values from -1 to 1
- step_upper: bfloat16 [2, 5, 5, 128, 32, 128], P(None, None, None, 'span', 'wall'), may hold values from -1 to 1
Outputs:
- response: float32 [2, 5, 4, 128, 32, 128], P(None, None, None, 'span', 'wall')
The draws below stay inside these ranges and needn't reach their ends.
All inputs are finite; a program needn't handle non-finite values.
Results may differ from the reference program's by a relative error of at most 0.0003.
Values may be sent and summed in bfloat16 or wider, within the bound.
No kernel may reach another device: no remote copies, remote signals or barrier semaphores. Data moves between devices by JAX's collectives and lax.ppermute only.
A program may use at most 128 MiB of HBM per device.

```python
import math
import jax
import jax.numpy as jnp
from jax import lax

FIELDS = 5
NZ = 128
NX = 128
COLS = 4
WALL_NORMAL_ROWS = 32


def decay_block(key):
    shape = (2, FIELDS, FIELDS, NZ, WALL_NORMAL_ROWS, NX)
    random_keys = jax.random.split(key, 7)
    slow_share = 0.5
    lane = (FIELDS, NZ, 1, NX)
    pick = jax.random.uniform(random_keys[0], lane)
    slow_rate = jax.random.uniform(random_keys[1], lane, minval=0.2, maxval=1.0) * (0.6 / WALL_NORMAL_ROWS)
    fast_rate = math.log(10.0) / jax.random.uniform(random_keys[2], lane, minval=30.0, maxval=50.0)
    growth_factor = jnp.where(pick < slow_share, slow_rate, fast_rate)
    height = jnp.arange(WALL_NORMAL_ROWS, dtype=jnp.float32).reshape(1, 1, WALL_NORMAL_ROWS, 1)
    growth_factor = growth_factor * (1.0 + height / WALL_NORMAL_ROWS)
    pulse_selection = jax.random.uniform(random_keys[3], (1, 1, WALL_NORMAL_ROWS, 1))
    pulse_length = jax.random.uniform(random_keys[4], (1, 1, WALL_NORMAL_ROWS, 1), minval=0.5, maxval=0.8)
    pulse_group = jnp.where(pulse_selection < 3.0 / WALL_NORMAL_ROWS, pulse_length, 1.0)
    forcing_amplitude = jnp.exp(-growth_factor - 0.01) * pulse_group
    phase = jax.random.uniform(random_keys[5], (FIELDS, NZ, WALL_NORMAL_ROWS, NX), minval=-math.pi, maxval=math.pi)
    coupling = jnp.clip(0.045 * jax.random.normal(random_keys[6], shape), -0.2, 0.2)
    unit = jnp.eye(FIELDS, dtype=jnp.float32).reshape(1, FIELDS, FIELDS, 1, 1, 1)
    diagonal = jnp.stack([forcing_amplitude * jnp.cos(phase), forcing_amplitude * jnp.sin(phase)])
    return coupling * (1.0 - unit) + diagonal[:, :, None] * unit


def draw_step_lower(key, part):
    return decay_block(jax.random.fold_in(key, 11)).astype(jnp.bfloat16)


def draw_step_upper(key, part):
    return decay_block(jax.random.fold_in(key, 29)).astype(jnp.bfloat16)


def block_levels(key, extent, cuts, least, top_value):
    loudness = 1.0
    for position, blocks in cuts:
        draws = jax.random.uniform(jax.random.fold_in(jax.random.fold_in(key, 6), position), (blocks,), jnp.float32, least / len(cuts), top_value / len(cuts))
        loudness = loudness * jnp.repeat(jnp.exp(draws), extent[position] // blocks).reshape((-1,) + (1,) * (len(extent) - 1 - position))
    return loudness


def noise(rng, dims, scale, most, cuts=(), kind=jnp.bfloat16):
    entries = jax.random.normal(rng, dims, jnp.float32) * scale
    if len(cuts) > 0:
        entries = block_levels(rng, dims, cuts, -0.22, 0.18) * entries
    return jnp.clip(entries, min=-most, max=most).astype(kind)


def setup_inputs(seed: int = 0) -> dict:
    splits = jax.random.split(jax.random.key(seed), 6)
    forcing = noise(splits[0], (2, FIELDS, COLS, NZ, WALL_NORMAL_ROWS, NX), 1.0, 6.0, ((3, 4), (4, 8)))
    span_factor = jnp.clip(jax.random.uniform(splits[1], (2, FIELDS, NZ), jnp.float32, -1.0, 1.0), -1.0, 1.0)
    pivot_inverse = noise(splits[2], (2, FIELDS, FIELDS, NZ, WALL_NORMAL_ROWS, NX), (1.0 / WALL_NORMAL_ROWS), 0.1875, ((3, 4), (4, 8)))
    step_lower = draw_step_lower(jax.random.fold_in(splits[5], 71), 0)
    step_upper = draw_step_upper(jax.random.fold_in(splits[5], 71), 0)
    return {"forcing": forcing, "span_factor": span_factor, "pivot_inverse": pivot_inverse, "step_lower": step_lower, "step_upper": step_upper}


exact_mode = lax.Precision.HIGHEST


def block_vector(matrix, vector):
    real = jnp.einsum("ijzx,jczx->iczx", matrix[0], vector[0], precision=exact_mode) - jnp.einsum("ijzx,jczx->iczx", matrix[1], vector[1], precision=exact_mode)
    imag = jnp.einsum("ijzx,jczx->iczx", matrix[0], vector[1], precision=exact_mode) + jnp.einsum("ijzx,jczx->iczx", matrix[1], vector[0], precision=exact_mode)
    return jnp.stack([real, imag])


def spectral_tables(count):
    modes = jnp.arange(count, dtype=jnp.int32)
    angle = ((modes[:, None] * modes[None, :]) % count).astype(jnp.float32) * (2.0 * math.pi / count)
    return jnp.cos(angle), jnp.sin(angle)


def reference(forcing, span_factor, pivot_inverse, step_lower, step_upper):
    cosine, sine = spectral_tables(NZ)

    def filter_field(inputs):
        field_re, field_im, factor = inputs
        field_re = field_re.astype(jnp.float32)
        field_im = field_im.astype(jnp.float32)
        spec_re = jnp.einsum("kz,qzyx->qkyx", cosine, field_re, precision=exact_mode) + jnp.einsum("kz,qzyx->qkyx", sine, field_im, precision=exact_mode)
        spec_im = jnp.einsum("kz,qzyx->qkyx", cosine, field_im, precision=exact_mode) - jnp.einsum("kz,qzyx->qkyx", sine, field_re, precision=exact_mode)
        factor_re = factor[0][None, :, None, None]
        factor_im = factor[1][None, :, None, None]
        filt_re = factor_re * spec_re - factor_im * spec_im
        filt_im = factor_re * spec_im + factor_im * spec_re
        back_re = (jnp.einsum("kz,qkyx->qzyx", cosine, filt_re, precision=exact_mode) - jnp.einsum("kz,qkyx->qzyx", sine, filt_im, precision=exact_mode)) / NZ
        back_im = (jnp.einsum("kz,qkyx->qzyx", cosine, filt_im, precision=exact_mode) + jnp.einsum("kz,qkyx->qzyx", sine, filt_re, precision=exact_mode)) / NZ
        return jnp.stack([back_re, back_im])

    driving = lax.map(filter_field, (forcing[0], forcing[1], jnp.transpose(span_factor, (1, 0, 2))))
    driving = jnp.transpose(driving, (1, 0, 2, 3, 4, 5))
    heights = jnp.arange(WALL_NORMAL_ROWS, dtype=jnp.int32)

    def forward_step(previous, height):
        pivot = lax.dynamic_index_in_dim(pivot_inverse, height, 4, False).astype(jnp.float32)
        lower = lax.dynamic_index_in_dim(step_lower, height, 4, False).astype(jnp.float32)
        source = lax.dynamic_index_in_dim(driving, height, 4, False)
        current = block_vector(pivot, source) - block_vector(lower, previous)
        return current, current

    start_state = jnp.zeros((2, FIELDS, COLS, NZ, NX), jnp.float32)
    sweep_rows = lax.scan(forward_step, start_state, heights)[1]

    def backward_step(following, inputs):
        height, sweep = inputs
        upper = lax.dynamic_index_in_dim(step_upper, height, 4, False).astype(jnp.float32)
        current = sweep - block_vector(upper, following)
        return current, current

    response_rows = lax.scan(backward_step, start_state, (heights, sweep_rows), reverse=True)[1]
    return jnp.moveaxis(response_rows, 0, 4)
```

```python
import functools
import math

import jax
import jax.numpy as jnp
from jax import lax
from jax.experimental import pallas as pl
from jax.experimental.pallas import tpu as pltpu
from jax.sharding import PartitionSpec as P

exact_mode = lax.Precision.HIGHEST
VMEM_LIMIT = 44 * 1024 * 1024
CHUNKS = ((0, 1), (2, 3))


def call(kernel, out_shape, scratch=(), flops=0, moved=0, **options):
    return pl.pallas_call(
        kernel,
        out_shape=out_shape,
        scratch_shapes=scratch,
        compiler_params=pltpu.CompilerParams(vmem_limit_bytes=VMEM_LIMIT),
        cost_estimate=pl.CostEstimate(flops=flops, bytes_accessed=moved, transcendentals=0),
        **options,
    )


def smem():
    return pl.BlockSpec(memory_space=pltpu.SMEM)


def vmem():
    return pl.BlockSpec(memory_space=pltpu.VMEM)


def f32(*shape):
    return jax.ShapeDtypeStruct(shape, jnp.float32)


def block_vector(matrix, vector):
    size = len(vector[0])
    real, imag = [], []
    for i in range(size):
        re = im = None
        for j in range(size):
            a, b = matrix(0, i, j), matrix(1, i, j)
            c, d = vector[0][j], vector[1][j]
            term_re, term_im = a * c - b * d, a * d + b * c
            re = term_re if re is None else re + term_re
            im = term_im if im is None else im + term_im
        real.append(re)
        imag.append(im)
    return [real, imag]


def plus(left, right):
    return [[a + b for a, b in zip(x, y)] for x, y in zip(left, right)]


def minus(left, right):
    return [[a - b for a, b in zip(x, y)] for x, y in zip(left, right)]


def negative(vector):
    return [[-a for a in x] for x in vector]


def load_vector(ref, size, *where):
    return [[ref[(r, i) + where] for i in range(size)] for r in range(2)]


def store_vector(ref, vector, *where):
    for r in range(2):
        for i, plane in enumerate(vector[r]):
            ref[(r, i) + where] = plane


def entry(ref, *lead, rows=slice(None)):
    return lambda r, i, j: ref[lead + (r, i, j, rows)].astype(jnp.float32)


def reorder_matrix(points, rows):
    size = points * rows
    to = lax.broadcasted_iota(jnp.int32, (size, size), 0)
    of = lax.broadcasted_iota(jnp.int32, (size, size), 1)
    wanted = (to % points) * rows + to // points
    return jnp.where(of == wanted, 1.0, 0.0).astype(jnp.bfloat16)


def repack_kernel(columns, rows, forcing_ref, *out_refs):
    parts, fields = forcing_ref.shape[:2]
    points = forcing_ref.shape[3] // rows
    order = reorder_matrix(points, rows)
    for place, column in enumerate(columns):
        for r in range(parts):
            for i in range(fields):
                moved = jnp.dot(
                    order, forcing_ref[r, i, place], preferred_element_type=jnp.float32
                ).astype(jnp.bfloat16)
                for y in range(rows):
                    out_refs[place][r, i, y] = moved[y * points : (y + 1) * points]


def prepare_kernel(
    rows,
    here_ref,
    pivot_ref,
    lower_ref,
    upper_ref,
    pivot_out,
    lower_out,
    upper_out,
    keep_ref,
    send_ref,
    held_ref,
):
    size = pivot_ref.shape[1]
    points = pivot_ref.shape[3] // rows
    half = points // 2
    order = reorder_matrix(points, rows)

    def move(index, carry):
        r, i = index // size, index % size
        for source, target in (
            (pivot_ref, pivot_out),
            (lower_ref, lower_out),
            (upper_ref, upper_out),
        ):
            for j in range(size):
                moved = jnp.dot(
                    order, source[r, i, j], preferred_element_type=jnp.float32
                ).astype(target.dtype)
                for y in range(rows):
                    target[y, r, i, j] = moved[y * points : (y + 1) * points]
        return carry

    lax.fori_loop(0, 2 * size, move, 0)

    core = here_ref[0]

    def summarize(index, carry):
        part, j = index // size, index % size
        span = pl.ds(part * half, half)

        def column(ref, y):
            return [
                [-ref[y, r, i, j, span].astype(jnp.float32) for i in range(size)]
                for r in range(2)
            ]

        def store(which, vector):
            @pl.when(part == core)
            def _():
                for r in range(2):
                    for i in range(size):
                        keep_ref[which, r, i, j] = vector[r][i]

            @pl.when(part != core)
            def _():
                for r in range(2):
                    for i in range(size):
                        send_ref[which, r, i, j] = vector[r][i]

        state = column(lower_out, 0)
        store_vector(held_ref.at[0], state)
        for y in range(1, rows):
            state = negative(block_vector(entry(lower_out, y, rows=span), state))
            store_vector(held_ref.at[y], state)
        store(0, state)
        for y in range(rows - 2, -1, -1):
            state = minus(
                load_vector(held_ref.at[y], size),
                block_vector(entry(upper_out, y, rows=span), state),
            )
        store(2, state)
        state = column(upper_out, rows - 1)
        for y in range(rows - 2, -1, -1):
            state = negative(block_vector(entry(upper_out, y, rows=span), state))
        store(1, state)
        return carry

    lax.fori_loop(0, 2 * size, summarize, 0)


def pair_matrices_kernel(here_ref, keep_ref, other_ref, pair_ref, chip_ref, joint_ref):
    core = here_ref[0]
    size = keep_ref.shape[2]
    for which in range(3):
        for r in range(2):
            for i in range(size):
                for j in range(size):
                    pair_ref[core, which, r, i, j] = keep_ref[which, r, i, j]
                    pair_ref[1 - core, which, r, i, j] = other_ref[which, r, i, j]

    def column(j, carry):
        def read(*lead):
            return [[pair_ref[lead + (r, i, j)] for i in range(size)] for r in range(2)]

        def write(ref, vector, *lead):
            for r in range(2):
                for i in range(size):
                    ref[lead + (r, i, j)] = vector[r][i]

        through = read(0, 0)
        write(chip_ref, block_vector(entry(pair_ref, 1, 0), through), 0)
        write(chip_ref, block_vector(entry(pair_ref, 0, 1), read(1, 1)), 1)
        joint = block_vector(entry(pair_ref, 1, 2), through)
        write(joint_ref, joint)
        write(chip_ref, plus(read(0, 2), block_vector(entry(pair_ref, 0, 1), joint)), 2)
        return carry

    lax.fori_loop(0, size, column, 0)


def upper_half_kernel(here_ref, chip_ref, beside_ref, out_ref):
    size = chip_ref.shape[2]

    @pl.when(here_ref[1] == 2)
    def _():
        def column(j, carry):
            state = [[chip_ref[0, r, i, j] for i in range(size)] for r in range(2)]
            state = block_vector(entry(beside_ref), state)
            state = block_vector(entry(chip_ref, 1), state)
            for r in range(2):
                for i in range(size):
                    out_ref[r, i, j] = chip_ref[2, r, i, j] + state[r][i]
            return carry

        lax.fori_loop(0, size, column, 0)

    @pl.when(here_ref[1] != 2)
    def _():
        out_ref[...] = jnp.zeros_like(out_ref)


def local_kernel(
    columns, sources, rows, here_ref, kernel_ref, pivot_ref, lower_ref, upper_ref, *refs
):
    arrived = refs[: columns * sources * 2]
    source_ref, keep_ref, send_ref, driving_ref, sweep_ref = refs[columns * sources * 2 :]
    size = pivot_ref.shape[2]
    points = pivot_ref.shape[4]
    half = points // 2
    for i in range(size):
        for c in range(columns):
            for y in range(0, rows, 2):
                right = jnp.concatenate(
                    [
                        jnp.concatenate(
                            [
                                arrived[(c * sources + m) * 2 + r][i, y + side]
                                for m in range(sources)
                                for r in range(2)
                            ],
                            axis=0,
                        )
                        for side in range(2)
                    ],
                    axis=1,
                )
                both = jnp.dot(kernel_ref[i], right, preferred_element_type=jnp.float32)
                total = both[: 2 * points] + both[2 * points :]
                for side in range(2):
                    lanes = slice(side * 128, (side + 1) * 128)
                    for r in range(2):
                        driving_ref[y + side, c, r, i] = total[
                            r * points : (r + 1) * points, lanes
                        ]
    core = here_ref[0]

    def solve(index, carry):
        part, c = index // columns, index % columns
        span = pl.ds(part * half, half)
        state = None
        for y in range(rows):
            source = block_vector(
                entry(pivot_ref, y, rows=span),
                load_vector(driving_ref.at[y, c], size, span),
            )
            store_vector(source_ref.at[y, c], source, span)
            if state is None:
                state = source
            else:
                state = minus(source, block_vector(entry(lower_ref, y, rows=span), state))
            store_vector(sweep_ref.at[y], state)
        back = state
        for y in range(rows - 2, -1, -1):
            back = minus(
                load_vector(sweep_ref.at[y], size),
                block_vector(entry(upper_ref, y, rows=span), back),
            )
        forth = load_vector(sweep_ref.at[rows - 1], size)

        @pl.when(part == core)
        def _():
            store_vector(keep_ref.at[0, c], forth)
            store_vector(keep_ref.at[1, c], back)

        @pl.when(part != core)
        def _():
            store_vector(send_ref.at[0, c], forth)
            store_vector(send_ref.at[1, c], back)

        return carry

    lax.fori_loop(0, 2 * columns, solve, 0)


def pair_kernel(
    columns, here_ref, pair_ref, keep_ref, other_ref, chip_ref, inner_ref, send_ref, both_ref
):
    core = here_ref[0]
    low = here_ref[1] < here_ref[2]
    size = pair_ref.shape[3]
    both_ref[core] = keep_ref[...]
    both_ref[1 - core] = other_ref[...]

    def column(c, carry):
        first = load_vector(both_ref.at[0, 0, c], size)
        forth = plus(
            load_vector(both_ref.at[1, 0, c], size), block_vector(entry(pair_ref, 1, 0), first)
        )
        entering = plus(
            load_vector(both_ref.at[1, 1, c], size), block_vector(entry(pair_ref, 1, 2), first)
        )
        back = plus(
            load_vector(both_ref.at[0, 1, c], size),
            block_vector(entry(pair_ref, 0, 1), entering),
        )
        store_vector(inner_ref.at[0, c], first)
        store_vector(inner_ref.at[1, c], entering)
        store_vector(chip_ref.at[0, c], forth)
        store_vector(chip_ref.at[1, c], back)

        @pl.when(low)
        def _():
            store_vector(send_ref.at[c], forth)

        @pl.when(jnp.logical_not(low))
        def _():
            store_vector(send_ref.at[c], back)

        return carry

    lax.fori_loop(0, columns, column, 0)


def halves_kernel(
    columns, here_ref, matrices_ref, beside_ref, chip_ref, came_ref, out_ref
):
    size = beside_ref.shape[1]
    chip = here_ref[1]

    @pl.when(chip == 1)
    def _():
        def column(c, carry):
            moved = block_vector(entry(matrices_ref, 0), load_vector(came_ref.at[c], size))
            store_vector(out_ref.at[c], plus(load_vector(chip_ref.at[0, c], size), moved))
            return carry

        lax.fori_loop(0, columns, column, 0)

    @pl.when(chip == 2)
    def _():
        def column(c, carry):
            forth = load_vector(chip_ref.at[0, c], size)
            moved = plus(load_vector(came_ref.at[c], size), block_vector(entry(beside_ref), forth))
            moved = block_vector(entry(matrices_ref, 1), moved)
            store_vector(out_ref.at[c], plus(load_vector(chip_ref.at[1, c], size), moved))
            return carry

        lax.fori_loop(0, columns, column, 0)

    @pl.when((chip == 0) | (chip == 3))
    def _():
        out_ref[...] = jnp.zeros_like(out_ref)


def middle_kernel(
    columns,
    here_ref,
    matrices_ref,
    beside_ref,
    upper_ref,
    chip_ref,
    first_ref,
    mine_ref,
    came_ref,
    edge_ref,
    out_ref,
):
    size = beside_ref.shape[1]
    chip = here_ref[1]

    @pl.when(chip == 1)
    def _():
        def column(c, carry):
            answer = plus(
                load_vector(came_ref.at[c], size),
                block_vector(entry(upper_ref), load_vector(mine_ref.at[c], size)),
            )
            store_vector(edge_ref.at[1, c], answer)
            onward = plus(
                load_vector(chip_ref.at[1, c], size), block_vector(entry(matrices_ref, 1), answer)
            )
            entering = load_vector(first_ref.at[c], size)
            store_vector(edge_ref.at[0, c], entering)
            store_vector(
                out_ref.at[c], plus(onward, block_vector(entry(matrices_ref, 2), entering))
            )
            return carry

        lax.fori_loop(0, columns, column, 0)

    @pl.when(chip == 2)
    def _():
        def column(c, carry):
            entering = load_vector(came_ref.at[c], size)
            store_vector(edge_ref.at[0, c], entering)
            onward = plus(
                load_vector(chip_ref.at[0, c], size),
                block_vector(entry(matrices_ref, 0), entering),
            )
            store_vector(out_ref.at[c], onward)
            store_vector(
                edge_ref.at[1, c],
                plus(
                    load_vector(first_ref.at[c], size), block_vector(entry(beside_ref), onward)
                ),
            )
            return carry

        lax.fori_loop(0, columns, column, 0)

    @pl.when((chip == 0) | (chip == 3))
    def _():
        edge_ref[...] = jnp.zeros_like(edge_ref)
        out_ref[...] = jnp.zeros_like(out_ref)


def split_kernel(
    columns, outer, here_ref, pair_ref, joint_ref, inner_ref, edge_ref, *refs
):
    came_ref = refs[0] if outer else None
    keep_ref, send_ref, entry_ref = refs[-3:]
    core, chip = here_ref[0], here_ref[1]
    size = pair_ref.shape[3]
    entry_ref[...] = edge_ref[...]
    if outer:

        @pl.when(chip == 0)
        def _():
            entry_ref[1] = came_ref[...]

        @pl.when(chip == 3)
        def _():
            entry_ref[0] = came_ref[...]

    def column(c, carry):
        sweep = load_vector(entry_ref.at[0, c], size)
        upper_sweep = plus(
            load_vector(inner_ref.at[0, c], size), block_vector(entry(pair_ref, 0, 0), sweep)
        )
        middle = plus(
            load_vector(inner_ref.at[1, c], size), block_vector(entry(joint_ref), sweep)
        )
        answer = load_vector(entry_ref.at[1, c], size)
        lower_answer = plus(middle, block_vector(entry(pair_ref, 1, 1), answer))

        def put(lower_target, upper_target):
            store_vector(lower_target.at[0, c], sweep)
            store_vector(lower_target.at[1, c], lower_answer)
            store_vector(upper_target.at[0, c], upper_sweep)
            store_vector(upper_target.at[1, c], answer)

        @pl.when(core == 0)
        def _():
            put(keep_ref, send_ref)

        @pl.when(core == 1)
        def _():
            put(send_ref, keep_ref)

        return carry

    lax.fori_loop(0, columns, column, 0)


def answer_kernel(
    columns, rows, here_ref, lower_ref, upper_ref, source_ref, keep_ref, other_ref, *refs
):
    out_ref, sweep_ref = refs[-2:]
    core = here_ref[0]
    size = lower_ref.shape[2]
    points = lower_ref.shape[4]
    half = points // 2

    def run(part, c, edge_ref):
        span = pl.ds(part * half, half)
        state = load_vector(edge_ref.at[0, c], size)
        for y in range(rows):
            state = minus(
                load_vector(source_ref.at[y, c], size, span),
                block_vector(entry(lower_ref, y, rows=span), state),
            )
            store_vector(sweep_ref.at[y], state)
        state = load_vector(edge_ref.at[1, c], size)
        for y in range(rows - 1, -1, -1):
            state = minus(
                load_vector(sweep_ref.at[y], size),
                block_vector(entry(upper_ref, y, rows=span), state),
            )
            place = pl.ds(part * (half * rows) + y, half, stride=rows)
            for r in range(2):
                for i in range(size):
                    out_ref[r, i, c, place] = state[r][i]

    def column(c, carry):
        run(core, c, keep_ref)
        run(1 - core, c, other_ref)
        return carry

    lax.fori_loop(0, columns, column, 0)


def span_kernel(span_factor, points, sources):
    count = span_factor.shape[2]
    modes = jnp.arange(count, dtype=jnp.int32)
    scale = 2.0 * math.pi / count
    angle_points = (points[:, None] * modes[None, :] % count).astype(jnp.float32) * scale
    cos_points = jnp.cos(angle_points)[None]
    sin_points = jnp.sin(angle_points)[None]
    factor_re = span_factor[0][:, None, :]
    factor_im = span_factor[1][:, None, :]
    left_re = factor_re * cos_points - factor_im * sin_points
    left_im = factor_re * sin_points + factor_im * cos_points
    flat = sources.reshape(-1)
    angle_modes = (modes[:, None] * flat[None, :] % count).astype(jnp.float32) * scale
    cos_modes = jnp.cos(angle_modes)
    sin_modes = jnp.sin(angle_modes)

    def product(left, right):
        return jnp.einsum("crk,kw->crw", left, right, precision=exact_mode)

    kernel_re = (product(left_re, cos_modes) + product(left_im, sin_modes)) / count
    kernel_im = (product(left_im, cos_modes) - product(left_re, sin_modes)) / count
    fields, own = kernel_re.shape[:2]
    split = (fields, own) + sources.shape
    kernel_re, kernel_im = kernel_re.reshape(split), kernel_im.reshape(split)
    real = jnp.stack([kernel_re, -kernel_im], axis=3)
    imag = jnp.stack([kernel_im, kernel_re], axis=3)
    whole = jnp.stack([real, imag], axis=1).reshape(fields, 2 * own, -1)
    high = lax.reduce_precision(whole, 8, 7)
    low = whole - high
    return jnp.concatenate([high, low], axis=1).astype(jnp.bfloat16)


def affine(matrix, vector, offset):
    left_re, left_im = matrix[0][None], matrix[1][None]
    right_re, right_im = vector[:, 0, None], vector[:, 1, None]
    real = jnp.sum(left_re * right_re - left_im * right_im, axis=2)
    imag = jnp.sum(left_re * right_im + left_im * right_re, axis=2)
    return offset + jnp.stack([real, imag], axis=1)


def local(forcing, span_factor, pivot_inverse, step_lower, step_upper):
    parts, fields, columns, points, rows, width = forcing.shape
    spans, walls = lax.axis_size("span"), lax.axis_size("wall")
    chips = walls // 2
    half = points // 2
    span_at, wall_at = lax.axis_index("span"), lax.axis_index("wall")
    here = jnp.stack([wall_at % 2, wall_at // 2, jnp.int32(chips // 2)]).astype(jnp.int32)

    flat = (points * rows, width)
    forcing = forcing.reshape(forcing.shape[:3] + flat)
    pivot_inverse = pivot_inverse.reshape(pivot_inverse.shape[:3] + flat)
    step_lower = step_lower.reshape(step_lower.shape[:3] + flat)
    step_upper = step_upper.reshape(step_upper.shape[:3] + flat)

    def swap(array, distance, axis):
        count = spans if axis == "span" else walls
        return lax.ppermute(array, axis, [(i, i ^ distance) for i in range(count)])

    block = jax.ShapeDtypeStruct((fields, rows, points, width), jnp.bfloat16)
    whole_block = jax.ShapeDtypeStruct((parts,) + block.shape, jnp.bfloat16)
    pieces = {}
    for chosen in CHUNKS:
        first = chosen[0]
        out = call(
            functools.partial(repack_kernel, chosen, rows),
            [whole_block] * len(chosen),
            moved=2 * forcing.size * 2 * len(chosen) // columns,
        )(lax.slice_in_dim(forcing, first, first + len(chosen), axis=2))
        for column, array in zip(chosen, out):
            pieces[column] = array
    arrived = {}
    for column in range(columns):
        mine = pieces[column]
        got = {0: mine}
        if spans == 4:
            got[1] = swap(mine, 1, "span")
            got[2] = swap(mine, 2, "span")
            if column % 2 == 0:
                got[3] = swap(got[2], 1, "span")
            else:
                got[3] = swap(got[1], 2, "span")
        else:
            for m in range(1, spans):
                got[m] = swap(mine, m, "span")
        arrived[column] = [got[m][r] for m in range(spans) for r in range(2)]

    own_points = span_at * points + jnp.arange(points, dtype=jnp.int32)
    partners = span_at ^ jnp.arange(spans, dtype=jnp.int32)
    source_points = partners[:, None] * points + jnp.arange(points, dtype=jnp.int32)[None]
    kernel = span_kernel(span_factor, own_points, source_points)

    kept = jnp.bfloat16 if half % 16 == 0 else jnp.float32
    moved_shape = jax.ShapeDtypeStruct((rows, 2, fields, fields, points, width), kept)
    plane = (half, width)
    summary = f32(3, 2, fields, fields, *plane)
    pivots, lowers, uppers, keep, send = call(
        functools.partial(prepare_kernel, rows),
        [moved_shape] * 3 + [summary] * 2,
        scratch=[pltpu.VMEM((rows, 2, fields) + plane, jnp.float32)],
        in_specs=[smem()] + [vmem()] * 3,
        flops=2 * 4500 * 8 * 1024,
        moved=12 * pivot_inverse.size,
    )(here, pivot_inverse, step_lower, step_upper)
    other = swap(send, 1, "wall")
    pair, chip_matrices, joint = call(
        pair_matrices_kernel,
        [
            f32(2, *summary.shape),
            summary,
            f32(2, fields, fields, *plane),
        ],
        in_specs=[smem()] + [vmem()] * 2,
        moved=4 * 6 * keep.size,
    )(here, keep, other)
    tree = chips == 4
    outward = [(i, i ^ 2) for i in range(walls)]
    inward = [(0, 1), (1, 0), (2, 4), (4, 2), (3, 5), (5, 3), (6, 7), (7, 6)]
    if tree:
        beside = lax.ppermute(chip_matrices[2], "wall", outward)
        upper_half = call(
            upper_half_kernel,
            f32(2, fields, fields, *plane),
            in_specs=[smem()] + [vmem()] * 2,
            moved=4 * 5 * keep.size // 3,
        )(here, chip_matrices, beside)
        upper_half = lax.ppermute(upper_half, "wall", inward)

    out = None
    for number, chosen in enumerate(CHUNKS):
        count = len(chosen)
        vectors = f32(2, count, 2, fields, *plane)
        single = f32(count, 2, fields, *plane)
        size = 2 * fields * count * half * width
        taken = [array for column in chosen for array in arrived[column]]
        source, keep, send = call(
            functools.partial(local_kernel, count, spans, rows),
            [f32(rows, count, 2, fields, points, width), vectors, vectors],
            scratch=[
                pltpu.VMEM((rows, count, 2, fields, points, width), jnp.float32),
                pltpu.VMEM((rows, 2, fields) + plane, jnp.float32),
            ],
            in_specs=[smem()] + [vmem()] * (4 + len(taken)),
            flops=2 * 400 * size,
            moved=6 * pivots.size + 4 * 16 * size,
        )(here, kernel, pivots, lowers, uppers, *taken)
        other = swap(send, 1, "wall")
        chip, inner, outgoing = call(
            functools.partial(pair_kernel, count),
            [vectors, vectors, single],
            scratch=[pltpu.VMEM((2,) + vectors.shape, jnp.float32)],
            in_specs=[smem()] + [vmem()] * 3,
            moved=4 * (pair.size + 9 * size),
        )(here, pair, keep, other)
        extra = ()
        if tree:
            came = lax.ppermute(outgoing, "wall", outward)
            mine = call(
                functools.partial(halves_kernel, count),
                single,
                in_specs=[smem()] + [vmem()] * 4,
                moved=4 * (chip_matrices.size + 4 * size),
            )(here, chip_matrices, beside, chip, came)
            across = lax.ppermute(mine, "wall", inward)
            edge, outgoing = call(
                functools.partial(middle_kernel, count),
                [vectors, single],
                in_specs=[smem()] + [vmem()] * 7,
                moved=4 * (chip_matrices.size + 8 * size),
            )(here, chip_matrices, beside, upper_half, chip, came, mine, across)
            extra = (lax.ppermute(outgoing, "wall", outward),)
        else:
            sweep = jnp.zeros(single.shape, jnp.float32)
            answer = jnp.zeros(single.shape, jnp.float32)
            upward = [(i, i + 2) for i in range(walls - 2)]
            downward = [(i + 2, i) for i in range(walls - 2)]
            for _ in range(chips - 1):
                sweep = lax.ppermute(affine(chip_matrices[0], sweep, chip[0]), "wall", upward)
            offset = affine(chip_matrices[2], sweep, chip[1])
            for _ in range(chips - 1):
                answer = lax.ppermute(affine(chip_matrices[1], answer, offset), "wall", downward)
            edge = jnp.stack([sweep, answer])
        keep, send = call(
            functools.partial(split_kernel, count, tree),
            [vectors, vectors],
            scratch=[pltpu.VMEM(vectors.shape, jnp.float32)],
            in_specs=[smem()] + [vmem()] * (4 + len(extra)),
            moved=4 * (pair.size + 9 * size),
        )(here, pair, joint, inner, edge, *extra)
        other = swap(send, 1, "wall")
        held = () if out is None else (out,)
        out = call(
            functools.partial(answer_kernel, count, rows),
            f32(2, fields, columns, *flat),
            scratch=[pltpu.VMEM((rows, 2, fields) + plane, jnp.float32)],
            grid=(1,),
            in_specs=[smem()] + [vmem()] * 5 + [pl.BlockSpec(memory_space=pl.ANY)] * len(held),
            out_specs=pl.BlockSpec(
                (2, fields, count) + flat,
                functools.partial(lambda at, step: (0, 0, at, 0, 0), chosen[0] // count),
            ),
            input_output_aliases={6: 0} if held else {},
            flops=2 * 400 * size,
            moved=4 * pivots.size + 4 * 24 * size,
        )(here, lowers, uppers, source, keep, other, *held)
    return out.reshape(2, fields, columns, points, rows, width)


def solution(mesh):
    placed = (
        P(None, None, None, "span", "wall", None),
        P(),
        P(None, None, None, "span", "wall", None),
        P(None, None, None, "span", "wall", None),
        P(None, None, None, "span", "wall", None),
    )
    return jax.shard_map(
        local,
        mesh=mesh,
        in_specs=placed,
        out_specs=P(None, None, None, "span", "wall", None),
        check_vma=False,
    )
```

```python
import functools
import math

import jax
import jax.numpy as jnp
from jax import lax
from jax.experimental import pallas as pl
from jax.experimental.pallas import tpu as pltpu
from jax.sharding import PartitionSpec as P

exact_mode = lax.Precision.HIGHEST
VMEM_LIMIT = 44 * 1024 * 1024
BYTES_PER_MICRO = 10_000
CHUNKS = ((0, 1), (2, 3))


def call(kernel, out_shape, scratch=(), micros=1.0, limit=VMEM_LIMIT, **options):
    plain = kernel.func if isinstance(kernel, functools.partial) else kernel
    return pl.pallas_call(
        kernel,
        name=plain.__name__,
        out_shape=out_shape,
        scratch_shapes=scratch,
        compiler_params=pltpu.CompilerParams(vmem_limit_bytes=limit),
        cost_estimate=pl.CostEstimate(
            flops=0, bytes_accessed=int(micros * BYTES_PER_MICRO), transcendentals=0
        ),
        **options,
    )


def vmem():
    return pl.BlockSpec(memory_space=pltpu.VMEM)


def f32(*shape):
    return jax.ShapeDtypeStruct(shape, jnp.float32)


def block_vectors(matrix, vectors):
    size = len(vectors[0][0])
    out = [([], []) for _ in vectors]
    for i in range(size):
        totals = [None] * len(vectors)
        for j in range(size):
            a, b = matrix(0, i, j), matrix(1, i, j)
            for place, vector in enumerate(vectors):
                c, d = vector[0][j], vector[1][j]
                term = (a * c - b * d, a * d + b * c)
                if j > 0:
                    term = (totals[place][0] + term[0], totals[place][1] + term[1])
                totals[place] = term
        for place, total in enumerate(totals):
            out[place][0].append(total[0])
            out[place][1].append(total[1])
    return out


def block_vector(matrix, vector):
    return block_vectors(matrix, [vector])[0]


def plus(left, right):
    return [[a + b for a, b in zip(x, y)] for x, y in zip(left, right)]


def minus(left, right):
    return [[a - b for a, b in zip(x, y)] for x, y in zip(left, right)]


def negative(vector):
    return [[-a for a in x] for x in vector]


def load_vector(ref, size, *where):
    return [[ref[(r, i) + where] for i in range(size)] for r in range(2)]


def store_vector(ref, vector, *where):
    for r in range(2):
        for i, plane in enumerate(vector[r]):
            ref[(r, i) + where] = plane


def entry(ref, *lead, rows=slice(None)):
    return lambda r, i, j: ref[lead + (r, i, j, rows)].astype(jnp.float32)


def reorder_matrix(points, rows, turn=0):
    size = points * rows
    to = lax.broadcasted_iota(jnp.int32, (size, size), 0)
    of = lax.broadcasted_iota(jnp.int32, (size, size), 1)
    wanted = (to % points) * rows + ((to // points) ^ turn)
    return jnp.where(of == wanted, 1.0, 0.0).astype(jnp.bfloat16)


def repack_kernel(rows, groups, forcing_ref, *out_refs):
    fields, columns = forcing_ref.shape[1:3]
    points = forcing_ref.shape[3] // rows
    each = columns // groups
    at = lax.axis_index("span")
    order = reorder_matrix(points, rows, at // groups)
    peak = jnp.zeros((points * rows, 256), jnp.float32)
    for r in range(2):
        for i in range(fields):
            for b in range(groups):
                for t in range(0, each, 2):
                    chosen = [
                        (t + side) * groups + (b ^ (at % groups)) if groups > 1 else t + side
                        for side in range(2)
                    ]
                    pair = jnp.concatenate(
                        [forcing_ref[r, i, column] for column in chosen], axis=1
                    )
                    moved = jnp.dot(order, pair, preferred_element_type=jnp.float32)
                    peak = jnp.maximum(peak, jnp.abs(moved))
                    moved = moved.astype(jnp.bfloat16)
                    for side in range(2):
                        plane = ((t + side) * 2 + r) * fields + i
                        for j in range(rows):
                            out_refs[j * groups + b][plane] = moved[
                                j * points : (j + 1) * points, side * 128 : (side + 1) * 128
                            ]
    peak = jnp.max(peak)
    for ref in out_refs:
        ref[each * 2 * fields] = jnp.full(ref.shape[1:], peak, jnp.float32).astype(jnp.bfloat16)


def filter_kernel(sources, kernel_ref, *refs):
    arrived, scale_ref, outs = refs[:sources], refs[sources], refs[sources + 1 :]
    each, fields, points = outs[0].shape[0], outs[0].shape[2], outs[0].shape[3]
    last = arrived[0].shape[0] - 1
    peak = arrived[0][last].astype(jnp.float32)
    for m in range(1, sources):
        peak = jnp.maximum(peak, arrived[m][last].astype(jnp.float32))
    peak = jnp.maximum(jnp.max(peak), 1e-30)
    scale = 2048.0 / jnp.full((8, 128), peak, jnp.float32)
    scale_ref[...] = jnp.full((8, 128), peak, jnp.float32) / 2048.0
    scale = jnp.max(scale)
    for i in range(fields):
        right = jnp.concatenate(
            [
                jnp.concatenate(
                    [
                        arrived[m][(t * 2 + r) * fields + i]
                        for m in range(sources)
                        for r in range(2)
                    ],
                    axis=0,
                )
                for t in range(each)
            ],
            axis=1,
        )
        both = jnp.dot(kernel_ref[i], right, preferred_element_type=jnp.float32)
        for m in range(sources):
            base = m * 4 * points
            total = (
                both[base : base + 2 * points] + both[base + 2 * points : base + 4 * points]
            ) * scale
            for t in range(each):
                for r in range(2):
                    outs[m][t, r, i] = total[
                        r * points : (r + 1) * points, t * 128 : (t + 1) * 128
                    ]


def reorder_kernel(rows, in_ref, after_ref, out_ref):
    size = in_ref.shape[1]
    points = in_ref.shape[3] // rows
    order = reorder_matrix(points, rows)

    def move(index, carry):
        r, i = index // size, index % size
        wide = jnp.concatenate([in_ref[r, i, j] for j in range(size)], axis=1)
        moved = jnp.dot(order, wide, preferred_element_type=jnp.float32).astype(out_ref.dtype)
        for j in range(size):
            for y in range(rows):
                out_ref[y, r, i, j] = moved[
                    y * points : (y + 1) * points, j * 128 : (j + 1) * 128
                ]
        return carry

    lax.fori_loop(0, 2 * size, move, 0)


def summary_kernel(rows, lower_ref, upper_ref, keep_ref, send_ref, held_ref):
    size = lower_ref.shape[2]
    half = lower_ref.shape[4] // 2
    core = lax.axis_index("wall") % 2

    def summarize(part, chosen):
        span = pl.ds(part * half, half)

        def column(ref, y):
            return [
                [
                    [-ref[y, r, i, j, span].astype(jnp.float32) for i in range(size)]
                    for r in range(2)
                ]
                for j in chosen
            ]

        def store(which, vectors):
            @pl.when(part == core)
            def _():
                for j, vector in zip(chosen, vectors):
                    for r in range(2):
                        for i in range(size):
                            keep_ref[which, r, i, j] = vector[r][i]

            @pl.when(part != core)
            def _():
                for j, vector in zip(chosen, vectors):
                    for r in range(2):
                        for i in range(size):
                            send_ref[which, r, i, j] = vector[r][i]

        states = column(lower_ref, 0)
        for place, state in enumerate(states):
            store_vector(held_ref.at[0, place], state)
        for y in range(1, rows):
            moved = block_vectors(entry(lower_ref, y, rows=span), states)
            states = [negative(move) for move in moved]
            for place, state in enumerate(states):
                store_vector(held_ref.at[y, place], state)
        store(0, states)
        for y in range(rows - 2, -1, -1):
            moved = block_vectors(entry(upper_ref, y, rows=span), states)
            states = [
                minus(load_vector(held_ref.at[y, place], size), move)
                for place, move in enumerate(moved)
            ]
        store(2, states)
        states = column(upper_ref, rows - 1)
        for y in range(rows - 2, -1, -1):
            moved = block_vectors(entry(upper_ref, y, rows=span), states)
            states = [negative(move) for move in moved]
        store(1, states)

    def half_of(part, carry):
        def pair(step, carry):
            summarize(part, [2 * step, 2 * step + 1])
            return carry

        lax.fori_loop(0, size // 2, pair, 0)
        if size % 2:
            summarize(part, [size - 1])
        return carry

    lax.fori_loop(0, 2, half_of, 0)


def pair_matrices_kernel(keep_ref, other_ref, pair_ref, chip_ref, joint_ref):
    core = lax.axis_index("wall") % 2
    size = keep_ref.shape[2]
    for which in range(3):
        for r in range(2):
            for i in range(size):
                for j in range(size):
                    pair_ref[core, which, r, i, j] = keep_ref[which, r, i, j]
                    pair_ref[1 - core, which, r, i, j] = other_ref[which, r, i, j]

    def column(j, carry):
        def read(*lead):
            return [[pair_ref[lead + (r, i, j)] for i in range(size)] for r in range(2)]

        def write(ref, vector, *lead):
            for r in range(2):
                for i in range(size):
                    ref[lead + (r, i, j)] = vector[r][i]

        through = read(0, 0)
        write(chip_ref, block_vector(entry(pair_ref, 1, 0), through), 0)
        write(chip_ref, block_vector(entry(pair_ref, 0, 1), read(1, 1)), 1)
        joint = block_vector(entry(pair_ref, 1, 2), through)
        write(joint_ref, joint)
        write(chip_ref, plus(read(0, 2), block_vector(entry(pair_ref, 0, 1), joint)), 2)
        return carry

    lax.fori_loop(0, size, column, 0)


def upper_half_kernel(chip_ref, beside_ref, out_ref):
    size = chip_ref.shape[2]

    chip = lax.axis_index("wall") // 2

    @pl.when(chip == 2)
    def _():
        def column(j, carry):
            state = [[chip_ref[0, r, i, j] for i in range(size)] for r in range(2)]
            state = block_vector(entry(beside_ref), state)
            state = block_vector(entry(chip_ref, 1), state)
            for r in range(2):
                for i in range(size):
                    out_ref[r, i, j] = chip_ref[2, r, i, j] + state[r][i]
            return carry

        lax.fori_loop(0, size, column, 0)

    @pl.when(chip != 2)
    def _():
        out_ref[...] = jnp.zeros_like(out_ref)


def local_kernel(
    columns, first, spans, rows, pivot_ref, lower_ref, upper_ref, scale_ref, *refs
):
    arrived = refs[:spans]
    source_ref, keep_ref, send_ref, driving_ref, sweep_ref = refs[spans:]
    size = pivot_ref.shape[2]
    points = pivot_ref.shape[4]
    half = points // 2
    groups = spans // rows
    at = lax.axis_index("span")
    scale = jnp.max(scale_ref[...])
    for m in range(spans):
        y = (m // groups) ^ (at // groups)
        for t in range(columns // groups):
            c = t * groups + ((m % groups) ^ (at % groups)) if groups > 1 else t
            driving_ref[y, c] = arrived[m][first // groups + t] * scale
    core = lax.axis_index("wall") % 2

    def solve(part, carry):
        span = pl.ds(part * half, half)
        states = None
        for y in range(rows):
            drivings = [load_vector(driving_ref.at[y, c], size, span) for c in range(columns)]
            news = block_vectors(entry(pivot_ref, y, rows=span), drivings)
            for c in range(columns):
                store_vector(source_ref.at[y, c], news[c], span)
            if states is not None:
                moved = block_vectors(entry(lower_ref, y, rows=span), states)
                news = [minus(new, move) for new, move in zip(news, moved)]
            states = news
            for c in range(columns):
                store_vector(sweep_ref.at[y, c], states[c])
        for y in range(rows - 2, -1, -1):
            moved = block_vectors(entry(upper_ref, y, rows=span), states)
            states = [
                minus(load_vector(sweep_ref.at[y, c], size), moved[c]) for c in range(columns)
            ]

        def put(ref):
            for c in range(columns):
                ref[0, c] = sweep_ref[rows - 1, c]
                store_vector(ref.at[1, c], states[c])

        @pl.when(part == core)
        def _():
            put(keep_ref)

        @pl.when(part != core)
        def _():
            put(send_ref)

        return carry

    lax.fori_loop(0, 2, solve, 0)


def pair_kernel(
    columns, chips, pair_ref, keep_ref, other_ref, chip_ref, inner_ref, send_ref, both_ref
):
    core = lax.axis_index("wall") % 2
    low = lax.axis_index("wall") // 2 < chips // 2
    size = pair_ref.shape[3]
    both_ref[core] = keep_ref[...]
    both_ref[1 - core] = other_ref[...]

    def column(c, carry):
        first = load_vector(both_ref.at[0, 0, c], size)
        forth = plus(
            load_vector(both_ref.at[1, 0, c], size), block_vector(entry(pair_ref, 1, 0), first)
        )
        entering = plus(
            load_vector(both_ref.at[1, 1, c], size), block_vector(entry(pair_ref, 1, 2), first)
        )
        back = plus(
            load_vector(both_ref.at[0, 1, c], size),
            block_vector(entry(pair_ref, 0, 1), entering),
        )
        store_vector(inner_ref.at[0, c], first)
        store_vector(inner_ref.at[1, c], entering)
        store_vector(chip_ref.at[0, c], forth)
        store_vector(chip_ref.at[1, c], back)

        @pl.when(low)
        def _():
            store_vector(send_ref.at[c], forth)

        @pl.when(jnp.logical_not(low))
        def _():
            store_vector(send_ref.at[c], back)

        return carry

    lax.fori_loop(0, columns, column, 0)


def halves_kernel(
    columns, matrices_ref, beside_ref, chip_ref, came_ref, out_ref
):
    size = beside_ref.shape[1]
    chip = lax.axis_index("wall") // 2

    @pl.when(chip == 1)
    def _():
        def column(c, carry):
            moved = block_vector(entry(matrices_ref, 0), load_vector(came_ref.at[c], size))
            store_vector(out_ref.at[c], plus(load_vector(chip_ref.at[0, c], size), moved))
            return carry

        lax.fori_loop(0, columns, column, 0)

    @pl.when(chip == 2)
    def _():
        def column(c, carry):
            forth = load_vector(chip_ref.at[0, c], size)
            moved = plus(load_vector(came_ref.at[c], size), block_vector(entry(beside_ref), forth))
            moved = block_vector(entry(matrices_ref, 1), moved)
            store_vector(out_ref.at[c], plus(load_vector(chip_ref.at[1, c], size), moved))
            return carry

        lax.fori_loop(0, columns, column, 0)

    @pl.when((chip == 0) | (chip == 3))
    def _():
        out_ref[...] = jnp.zeros_like(out_ref)


def middle_kernel(
    columns,
    matrices_ref,
    beside_ref,
    upper_ref,
    chip_ref,
    first_ref,
    mine_ref,
    came_ref,
    edge_ref,
    out_ref,
):
    size = beside_ref.shape[1]
    chip = lax.axis_index("wall") // 2

    @pl.when(chip == 1)
    def _():
        def column(c, carry):
            answer = plus(
                load_vector(came_ref.at[c], size),
                block_vector(entry(upper_ref), load_vector(mine_ref.at[c], size)),
            )
            store_vector(edge_ref.at[1, c], answer)
            onward = plus(
                load_vector(chip_ref.at[1, c], size), block_vector(entry(matrices_ref, 1), answer)
            )
            entering = load_vector(first_ref.at[c], size)
            store_vector(edge_ref.at[0, c], entering)
            store_vector(
                out_ref.at[c], plus(onward, block_vector(entry(matrices_ref, 2), entering))
            )
            return carry

        lax.fori_loop(0, columns, column, 0)

    @pl.when(chip == 2)
    def _():
        def column(c, carry):
            entering = load_vector(came_ref.at[c], size)
            store_vector(edge_ref.at[0, c], entering)
            onward = plus(
                load_vector(chip_ref.at[0, c], size),
                block_vector(entry(matrices_ref, 0), entering),
            )
            store_vector(out_ref.at[c], onward)
            store_vector(
                edge_ref.at[1, c],
                plus(
                    load_vector(first_ref.at[c], size), block_vector(entry(beside_ref), onward)
                ),
            )
            return carry

        lax.fori_loop(0, columns, column, 0)

    @pl.when((chip == 0) | (chip == 3))
    def _():
        edge_ref[...] = jnp.zeros_like(edge_ref)
        out_ref[...] = jnp.zeros_like(out_ref)


def split_kernel(
    columns, outer, pair_ref, joint_ref, inner_ref, edge_ref, *refs
):
    came_ref = refs[0] if outer else None
    keep_ref, send_ref, entry_ref = refs[-3:]
    core, chip = lax.axis_index("wall") % 2, lax.axis_index("wall") // 2
    size = pair_ref.shape[3]
    entry_ref[...] = edge_ref[...]
    if outer:

        @pl.when(chip == 0)
        def _():
            entry_ref[1] = came_ref[...]

        @pl.when(chip == 3)
        def _():
            entry_ref[0] = came_ref[...]

    def column(c, carry):
        sweep = load_vector(entry_ref.at[0, c], size)
        upper_sweep = plus(
            load_vector(inner_ref.at[0, c], size), block_vector(entry(pair_ref, 0, 0), sweep)
        )
        middle = plus(
            load_vector(inner_ref.at[1, c], size), block_vector(entry(joint_ref), sweep)
        )
        answer = load_vector(entry_ref.at[1, c], size)
        lower_answer = plus(middle, block_vector(entry(pair_ref, 1, 1), answer))

        def put(lower_target, upper_target):
            store_vector(lower_target.at[0, c], sweep)
            store_vector(lower_target.at[1, c], lower_answer)
            store_vector(upper_target.at[0, c], upper_sweep)
            store_vector(upper_target.at[1, c], answer)

        @pl.when(core == 0)
        def _():
            put(keep_ref, send_ref)

        @pl.when(core == 1)
        def _():
            put(send_ref, keep_ref)

        return carry

    lax.fori_loop(0, columns, column, 0)


def answer_kernel(
    columns, first, rows, lower_ref, upper_ref, source_ref, keep_ref, other_ref, *refs
):
    out_ref, sweep_ref, edge_ref, made_ref, done = refs[-5:]
    core = lax.axis_index("wall") % 2
    size = lower_ref.shape[2]
    points = lower_ref.shape[4]
    half = points // 2
    edge_ref[core] = keep_ref[...]
    edge_ref[1 - core] = other_ref[...]

    def copies(part):
        return [
            pltpu.make_async_copy(
                made_ref.at[part, r, i],
                out_ref.at[
                    r, i, pl.ds(first, columns), pl.ds(part * half * rows, half * rows)
                ],
                done.at[part, r, i],
            )
            for r in range(2)
            for i in range(size)
        ]

    def run(part, carry):
        span = pl.ds(part * half, half)
        states = [load_vector(edge_ref.at[part, 0, c], size) for c in range(columns)]
        for y in range(rows):
            moved = block_vectors(entry(lower_ref, y, rows=span), states)
            states = [
                minus(load_vector(source_ref.at[y, c], size, span), moved[c])
                for c in range(columns)
            ]
            for c in range(columns):
                store_vector(sweep_ref.at[y, c], states[c])
        states = [load_vector(edge_ref.at[part, 1, c], size) for c in range(columns)]
        for y in range(rows - 1, -1, -1):
            moved = block_vectors(entry(upper_ref, y, rows=span), states)
            states = [
                minus(load_vector(sweep_ref.at[y, c], size), moved[c]) for c in range(columns)
            ]
            place = pl.ds(y, half, stride=rows)
            for c in range(columns):
                for r in range(2):
                    for i in range(size):
                        made_ref[part, r, i, c, place] = states[c][r][i]
        for copy in copies(part):
            copy.start()
        return carry

    lax.fori_loop(0, 2, run, 0)
    for copy in copies(0) + copies(1):
        copy.wait()


def span_kernel(span_factor, own, span_at):
    count = span_factor.shape[2]
    fields = span_factor.shape[1]
    slot = jnp.arange(count, dtype=jnp.int32)
    points = (span_at ^ (slot // own)) * own + slot % own
    modes = jnp.arange(count, dtype=jnp.int32)
    scale = 2.0 * math.pi / count
    angle_points = (points[:, None] * modes[None, :] % count).astype(jnp.float32) * scale
    cos_points = jnp.cos(angle_points)[None]
    sin_points = jnp.sin(angle_points)[None]
    factor_re = span_factor[0][:, None, :] / count
    factor_im = span_factor[1][:, None, :] / count
    left_re = factor_re * cos_points - factor_im * sin_points
    left_im = factor_re * sin_points + factor_im * cos_points
    spans = count // own
    left = jnp.stack(
        [
            jnp.concatenate([left_re, left_im], axis=2).reshape(fields, spans, own, 2 * count),
            jnp.concatenate([left_im, -left_re], axis=2).reshape(fields, spans, own, 2 * count),
        ],
        axis=2,
    ).reshape(fields * 2 * count, 2 * count)
    quarter = count // 4
    column = jnp.arange(2 * count, dtype=jnp.int32)
    place = (span_at ^ (column // (2 * own))) * own + column % own
    turn = (column // own) % 2 * quarter
    steps = (modes[:, None] * place[None, :] + (count - turn)[None, :]) % count
    angle = steps.astype(jnp.float32) * scale
    right = jnp.concatenate([jnp.cos(angle), jnp.sin(angle)], axis=0)
    whole = jnp.dot(left, right, precision=exact_mode).reshape(fields, spans, 2 * own, -1)
    high = lax.reduce_precision(whole, 8, 7)
    low = whole - high
    both = jnp.concatenate([high, low], axis=2).astype(jnp.bfloat16)
    return both.reshape(fields, 4 * count, -1)


def affine(matrix, vector, offset):
    left_re, left_im = matrix[0][None], matrix[1][None]
    right_re, right_im = vector[:, 0, None], vector[:, 1, None]
    real = jnp.sum(left_re * right_re - left_im * right_im, axis=2)
    imag = jnp.sum(left_re * right_im + left_im * right_re, axis=2)
    return offset + jnp.stack([real, imag], axis=1)


def local(forcing, span_factor, pivot_inverse, step_lower, step_upper):
    parts, fields, columns, points, rows, width = forcing.shape
    spans, walls = lax.axis_size("span"), lax.axis_size("wall")
    chips = walls // 2
    half = points // 2
    span_at = lax.axis_index("span")

    flat = (points * rows, width)
    forcing = forcing.reshape(forcing.shape[:3] + flat)
    pivot_inverse = pivot_inverse.reshape(pivot_inverse.shape[:3] + flat)
    step_lower = step_lower.reshape(step_lower.shape[:3] + flat)
    step_upper = step_upper.reshape(step_upper.shape[:3] + flat)

    def swap(array, distance, axis, name):
        count = spans if axis == "span" else walls
        with jax.named_scope(name):
            return lax.ppermute(array, axis, [(i, i ^ distance) for i in range(count)])

    def gate(array, *earlier):
        return lax.optimization_barrier((array,) + earlier)[0]

    groups = spans // rows
    kernel = span_kernel(span_factor, points, span_at)
    block = (columns // groups * 2 * fields + 1, points, width)
    sent = call(
        functools.partial(repack_kernel, rows, groups),
        [jax.ShapeDtypeStruct(block, jnp.bfloat16)] * spans,
        micros=2.0,
        in_specs=[vmem()],
    )(forcing)
    sent = [sent[0]] + [
        swap(sent[m], m, "span", f"forcing{m}") for m in range(1, spans)
    ]

    kept = jnp.bfloat16 if half % 16 == 0 else jnp.float32
    moved_shape = jax.ShapeDtypeStruct((rows, 2, fields, fields, points, width), kept)
    plane = (half, width)
    summary = f32(3, 2, fields, fields, *plane)
    def reorder(matrix, after):
        return call(
            functools.partial(reorder_kernel, rows),
            moved_shape,
            micros=2.0,
            in_specs=[vmem(), pl.BlockSpec(memory_space=pl.ANY)],
        )(matrix, after)

    lowers, uppers = reorder(step_lower, sent[0]), reorder(step_upper, sent[0])
    keep, send = call(
        functools.partial(summary_kernel, rows),
        [summary] * 2,
            micros=8.2,
        scratch=[pltpu.VMEM((rows, 2, 2, fields) + plane, jnp.float32)],
        in_specs=[vmem()] * 2,
    )(lowers, uppers)
    scale, *outs = call(
        functools.partial(filter_kernel, spans),
        [f32(8, 128)] + [f32(columns // groups, 2, fields, points, width)] * spans,
        micros=1.0,
    )(gate(kernel, keep), *sent)
    drivings = [outs[0]] + [
        swap(outs[m].astype(jnp.float16), m, "span", f"driving{m}").astype(jnp.float32)
        for m in range(1, spans)
    ]

    pivots = reorder(pivot_inverse, outs[0])
    other = swap(send, 1, "wall", "matrices_core")
    pair, chip_matrices, joint = call(
        pair_matrices_kernel,
        [
            f32(2, *summary.shape),
            summary,
            f32(2, fields, fields, *plane),
        ],
            micros=3.6,
        in_specs=[vmem()] * 2,
    )(gate(keep, drivings[1]), other)
    tree = chips == 4
    outward = [(i, i ^ 2) for i in range(walls)]
    inward = [(0, 1), (1, 0), (2, 4), (4, 2), (3, 5), (5, 3), (6, 7), (7, 6)]
    if tree:
        with jax.named_scope("matrices_outward"):
            beside = lax.ppermute(chip_matrices[2], "wall", outward)

    out = None
    for number, chosen in enumerate(CHUNKS):
        count = len(chosen)
        vectors = f32(2, count, 2, fields, *plane)
        single = f32(count, 2, fields, *plane)
        size = 2 * fields * count * half * width
        taken = drivings
        source, keep, send = call(
            functools.partial(local_kernel, count, chosen[0], spans, rows),
            [f32(rows, count, 2, fields, points, width), vectors, vectors],
            micros=2.2 * count,
            scratch=[
                pltpu.VMEM((rows, count, 2, fields, points, width), jnp.float32),
                pltpu.VMEM((rows, count, 2, fields) + plane, jnp.float32),
            ],
            in_specs=[vmem()] * (4 + len(taken)),
        )(pivots, lowers, uppers, scale, *taken)
        other = swap(send, 1, "wall", f"chunk{number}_core")
        chip, inner, outgoing = call(
            functools.partial(pair_kernel, count, chips),
            [vectors, vectors, single],
            micros=0.5 * count,
            scratch=[pltpu.VMEM((2,) + vectors.shape, jnp.float32)],
            in_specs=[vmem()] * 3,
        )(pair, keep, other)
        extra = ()
        if tree and number == 0:
            upper_half = call(
                upper_half_kernel,
                f32(2, fields, fields, *plane),
                micros=0.7,
                in_specs=[vmem()] * 2,
            )(gate(chip_matrices, outgoing), beside)
            with jax.named_scope("matrices_inward"):
                upper_half = lax.ppermute(upper_half, "wall", inward)
        if tree:
            with jax.named_scope(f"chunk{number}_to_middle"):
                came = lax.ppermute(outgoing, "wall", outward)
            mine = call(
                functools.partial(halves_kernel, count),
                single,
            micros=0.3 * count,
                in_specs=[vmem()] * 4,
            )(chip_matrices, beside, chip, came)
            with jax.named_scope(f"chunk{number}_middle"):
                across = lax.ppermute(mine, "wall", inward)
            edge, outgoing = call(
                functools.partial(middle_kernel, count),
                [vectors, single],
            micros=0.3 * count,
                in_specs=[vmem()] * 7,
            )(chip_matrices, beside, upper_half, chip, came, mine, across)
            with jax.named_scope(f"chunk{number}_to_ends"):
                extra = (lax.ppermute(outgoing, "wall", outward),)
        else:
            sweep = jnp.zeros(single.shape, jnp.float32)
            answer = jnp.zeros(single.shape, jnp.float32)
            upward = [(i, i + 2) for i in range(walls - 2)]
            downward = [(i + 2, i) for i in range(walls - 2)]
            for _ in range(chips - 1):
                sweep = lax.ppermute(affine(chip_matrices[0], sweep, chip[0]), "wall", upward)
            offset = affine(chip_matrices[2], sweep, chip[1])
            for _ in range(chips - 1):
                answer = lax.ppermute(affine(chip_matrices[1], answer, offset), "wall", downward)
            edge = jnp.stack([sweep, answer])
        keep, send = call(
            functools.partial(split_kernel, count, tree),
            [vectors, vectors],
            micros=0.5 * count,
            scratch=[pltpu.VMEM(vectors.shape, jnp.float32)],
            in_specs=[vmem()] * (4 + len(extra)),
        )(pair, joint, inner, edge, *extra)
        other = swap(send, 1, "wall", f"chunk{number}_apart")
        held = () if out is None else (out,)
        out = call(
            functools.partial(answer_kernel, count, chosen[0], rows),
            f32(2, fields, columns, *flat),
            micros=1.2 * count,
            scratch=[
                pltpu.VMEM((rows, count, 2, fields) + plane, jnp.float32),
                pltpu.VMEM((2,) + vectors.shape, jnp.float32),
                pltpu.VMEM((2, 2, fields, count, half * rows, width), jnp.float32),
                pltpu.SemaphoreType.DMA((2, 2, fields)),
            ],
            in_specs=[vmem()] * 5 + [pl.BlockSpec(memory_space=pl.ANY)] * len(held),
            out_specs=pl.BlockSpec(memory_space=pl.ANY),
            input_output_aliases={5: 0} if held else {},
        )(lowers, uppers, source, keep, other, *held)
    return out.reshape(2, fields, columns, points, rows, width)


def solution(mesh):
    placed = (
        P(None, None, None, "span", "wall", None),
        P(),
        P(None, None, None, "span", "wall", None),
        P(None, None, None, "span", "wall", None),
        P(None, None, None, "span", "wall", None),
    )
    return jax.shard_map(
        local,
        mesh=mesh,
        in_specs=placed,
        out_specs=P(None, None, None, "span", "wall", None),
        check_vma=False,
    )
```

```python
import functools
import math

import jax
import jax.numpy as jnp
from jax import lax
from jax.experimental import pallas as pl
from jax.experimental.pallas import tpu as pltpu
from jax.sharding import PartitionSpec as P

exact_mode = lax.Precision.HIGHEST
VMEM_LIMIT = 24 * 1024 * 1024
BYTES_PER_MICRO = 3_600_000
CHUNKS = ((0, 1), (2, 3))


def call(kernel, out_shape, scratch=(), micros=1.0, limit=VMEM_LIMIT, **options):
    plain = kernel.func if isinstance(kernel, functools.partial) else kernel
    return pl.pallas_call(
        kernel,
        name=plain.__name__,
        out_shape=out_shape,
        scratch_shapes=scratch,
        compiler_params=pltpu.CompilerParams(vmem_limit_bytes=limit),
        cost_estimate=pl.CostEstimate(
            flops=0, bytes_accessed=int(micros * BYTES_PER_MICRO), transcendentals=0
        ),
        **options,
    )


def vmem():
    return pl.BlockSpec(memory_space=pltpu.VMEM)


def anywhere():
    return pl.BlockSpec(memory_space=pl.ANY)


def f32(*shape):
    return jax.ShapeDtypeStruct(shape, jnp.float32)


def block_vectors(matrix, vectors):
    size = len(vectors[0][0])
    out = [([], []) for _ in vectors]
    for i in range(size):
        totals = [None] * len(vectors)
        for j in range(size):
            a, b = matrix(0, i, j), matrix(1, i, j)
            for place, vector in enumerate(vectors):
                c, d = vector[0][j], vector[1][j]
                term = (a * c - b * d, a * d + b * c)
                if j > 0:
                    term = (totals[place][0] + term[0], totals[place][1] + term[1])
                totals[place] = term
        for place, total in enumerate(totals):
            out[place][0].append(total[0])
            out[place][1].append(total[1])
    return out


def block_vector(matrix, vector):
    return block_vectors(matrix, [vector])[0]


def plus(left, right):
    return [[a + b for a, b in zip(x, y)] for x, y in zip(left, right)]


def minus(left, right):
    return [[a - b for a, b in zip(x, y)] for x, y in zip(left, right)]


def negative(vector):
    return [[-a for a in x] for x in vector]


def load_vector(ref, size, *where):
    return [[ref[(r, i) + where] for i in range(size)] for r in range(2)]


def store_vector(ref, vector, *where):
    for r in range(2):
        for i, plane in enumerate(vector[r]):
            ref[(r, i) + where] = plane


def entry(ref, *lead, rows=slice(None)):
    return lambda r, i, j: ref[lead + (r, i, j, rows)].astype(jnp.float32)


def reorder_matrix(points, rows, turn=0):
    size = points * rows
    to = lax.broadcasted_iota(jnp.int32, (size, size), 0)
    of = lax.broadcasted_iota(jnp.int32, (size, size), 1)
    wanted = (to % points) * rows + ((to // points) ^ turn)
    return jnp.where(of == wanted, 1.0, 0.0).astype(jnp.bfloat16)


def repack_kernel(rows, groups, forcing_ref, mark_ref, *out_refs):
    fields, columns = forcing_ref.shape[1:3]
    points = forcing_ref.shape[3] // rows
    each = columns // groups
    at = lax.axis_index("span")
    order = reorder_matrix(points, rows, at // groups)
    peak = jnp.zeros((points * rows, 256), jnp.float32)
    for r in range(2):
        for i in range(fields):
            for b in range(groups):
                for t in range(0, each, 2):
                    chosen = [
                        (t + side) * groups + (b ^ (at % groups)) if groups > 1 else t + side
                        for side in range(2)
                    ]
                    pair = jnp.concatenate(
                        [forcing_ref[r, i, column] for column in chosen], axis=1
                    )
                    moved = jnp.dot(order, pair, preferred_element_type=jnp.float32)
                    peak = jnp.maximum(peak, jnp.abs(moved))
                    moved = moved.astype(jnp.bfloat16)
                    for side in range(2):
                        plane = ((t + side) * 2 + r) * fields + i
                        for j in range(rows):
                            out_refs[j * groups + b][plane] = moved[
                                j * points : (j + 1) * points, side * 128 : (side + 1) * 128
                            ]
    peak = jnp.max(peak)
    mark_ref[...] = jnp.zeros_like(mark_ref)
    for ref in out_refs:
        ref[each * 2 * fields] = jnp.full(ref.shape[1:], peak, jnp.float32).astype(jnp.bfloat16)


def table_kernel(own, factor_ref, after_ref, out_ref):
    fields, count = factor_ref.shape[1:]
    at = lax.axis_index("span")
    scale = 2.0 * math.pi / count

    def grid(shape, dimension):
        return lax.broadcasted_iota(jnp.int32, shape, dimension)

    def point(slot):
        return (at ^ (slot // own)) * own + slot % own

    wide = (count, 2 * count)
    column = grid(wide, 1)
    source = point((column // (2 * own)) * own + column % own)
    turn = (column // own) % 2 * (count // 4)
    steps = (grid(wide, 0) * source + count - turn) % count
    angle = steps.astype(jnp.float32) * scale
    right = jnp.concatenate([jnp.cos(angle), jnp.sin(angle)], axis=0)
    square = (count, count)
    angle = (point(grid(square, 0)) * grid(square, 1) % count).astype(jnp.float32) * scale
    cosine, sine = jnp.cos(angle) / count, jnp.sin(angle) / count
    for i in range(fields):
        factor_re, factor_im = factor_ref[0, i : i + 1], factor_ref[1, i : i + 1]
        left_re = factor_re * cosine - factor_im * sine
        left_im = factor_re * sine + factor_im * cosine
        for part, left in enumerate(([left_re, left_im], [left_im, -left_re])):
            whole = jnp.dot(
                jnp.concatenate(left, axis=1),
                right,
                precision=exact_mode,
                preferred_element_type=jnp.float32,
            )
            high = whole.astype(jnp.bfloat16)
            low = (whole - high.astype(jnp.float32)).astype(jnp.bfloat16)
            for m in range(count // own):
                base = (4 * m + part) * own
                rows = slice(m * own, (m + 1) * own)
                out_ref[i, base : base + own] = high[rows]
                out_ref[i, base + 2 * own : base + 3 * own] = low[rows]


def filter_kernel(sources, chunks, kernel_ref, *refs):
    arrived, scale_ref, outs = refs[:sources], refs[sources], refs[sources + 1 :]
    each, fields, points = outs[0].shape[0] * chunks, outs[0].shape[2], outs[0].shape[3]
    last = arrived[0].shape[0] - 1
    peak = arrived[0][last].astype(jnp.float32)
    for m in range(1, sources):
        peak = jnp.maximum(peak, arrived[m][last].astype(jnp.float32))
    peak = jnp.maximum(jnp.max(peak), 1e-30)
    scale = 2048.0 / jnp.full((8, 128), peak, jnp.float32)
    scale_ref[...] = jnp.full((8, 128), peak, jnp.float32) / 2048.0
    scale = jnp.max(scale)
    for i in range(fields):
        right = jnp.concatenate(
            [
                jnp.concatenate(
                    [
                        arrived[m][(t * 2 + r) * fields + i]
                        for m in range(sources)
                        for r in range(2)
                    ],
                    axis=0,
                )
                for t in range(each)
            ],
            axis=1,
        )
        both = jnp.dot(kernel_ref[i], right, preferred_element_type=jnp.float32)
        for m in range(sources):
            base = m * 4 * points
            total = (
                both[base : base + 2 * points] + both[base + 2 * points : base + 4 * points]
            ) * scale
            for t in range(each):
                for r in range(2):
                    outs[t * chunks // each * sources + m][t % (each // chunks), r, i] = total[
                        r * points : (r + 1) * points, t * 128 : (t + 1) * 128
                    ]


def reorder_kernel(rows, in_ref, after_ref, out_ref):
    size = in_ref.shape[1]
    points = in_ref.shape[3] // rows
    order = reorder_matrix(points, rows)

    def move(index, carry):
        r, i = index // size, index % size
        wide = jnp.concatenate([in_ref[r, i, j] for j in range(size)], axis=1)
        moved = jnp.dot(order, wide, preferred_element_type=jnp.float32).astype(out_ref.dtype)
        for j in range(size):
            for y in range(rows):
                out_ref[y, r, i, j] = moved[
                    y * points : (y + 1) * points, j * 128 : (j + 1) * 128
                ]
        return carry

    lax.fori_loop(0, 2 * size, move, 0)


def summary_kernel(rows, lower_ref, upper_ref, mark_ref, keep_ref, send_ref, held_ref):
    size = lower_ref.shape[2]
    half = lower_ref.shape[4] // 2
    core = lax.axis_index("wall") % 2
    mark_ref[...] = jnp.zeros_like(mark_ref)

    def summarize(part, chosen):
        span = pl.ds(part * half, half)

        def column(ref, y):
            return [
                [
                    [-ref[y, r, i, j, span].astype(jnp.float32) for i in range(size)]
                    for r in range(2)
                ]
                for j in chosen
            ]

        def store(which, vectors):
            @pl.when(part == core)
            def _():
                for j, vector in zip(chosen, vectors):
                    for r in range(2):
                        for i in range(size):
                            keep_ref[which, r, i, j] = vector[r][i]

            @pl.when(part != core)
            def _():
                for j, vector in zip(chosen, vectors):
                    for r in range(2):
                        for i in range(size):
                            send_ref[which, r, i, j] = vector[r][i]

        states = column(lower_ref, 0)
        for place, state in enumerate(states):
            store_vector(held_ref.at[0, place], state)
        for y in range(1, rows):
            moved = block_vectors(entry(lower_ref, y, rows=span), states)
            states = [negative(move) for move in moved]
            for place, state in enumerate(states):
                store_vector(held_ref.at[y, place], state)
        store(0, states)
        for y in range(rows - 2, -1, -1):
            moved = block_vectors(entry(upper_ref, y, rows=span), states)
            states = [
                minus(load_vector(held_ref.at[y, place], size), move)
                for place, move in enumerate(moved)
            ]
        store(2, states)
        states = column(upper_ref, rows - 1)
        for y in range(rows - 2, -1, -1):
            moved = block_vectors(entry(upper_ref, y, rows=span), states)
            states = [negative(move) for move in moved]
        store(1, states)

    def half_of(part, carry):
        def pair(step, carry):
            summarize(part, [2 * step, 2 * step + 1])
            return carry

        lax.fori_loop(0, size // 2, pair, 0)
        if size % 2:
            summarize(part, [size - 1])
        return carry

    lax.fori_loop(0, 2, half_of, 0)


def pair_matrices_kernel(after_ref, keep_ref, other_ref, pair_ref, chip_ref, joint_ref):
    core = lax.axis_index("wall") % 2
    size = keep_ref.shape[2]
    for which in range(3):
        for r in range(2):
            for i in range(size):
                for j in range(size):
                    pair_ref[core, which, r, i, j] = keep_ref[which, r, i, j]
                    pair_ref[1 - core, which, r, i, j] = other_ref[which, r, i, j]

    def column(j, carry):
        def read(*lead):
            return [[pair_ref[lead + (r, i, j)] for i in range(size)] for r in range(2)]

        def write(ref, vector, *lead):
            for r in range(2):
                for i in range(size):
                    ref[lead + (r, i, j)] = vector[r][i]

        through = read(0, 0)
        write(chip_ref, block_vector(entry(pair_ref, 1, 0), through), 0)
        write(chip_ref, block_vector(entry(pair_ref, 0, 1), read(1, 1)), 1)
        joint = block_vector(entry(pair_ref, 1, 2), through)
        write(joint_ref, joint)
        write(chip_ref, plus(read(0, 2), block_vector(entry(pair_ref, 0, 1), joint)), 2)
        return carry

    lax.fori_loop(0, size, column, 0)


def upper_half_kernel(*refs):
    chip_ref, beside_ref, out_ref = refs[-3:]
    size = chip_ref.shape[2]

    chip = lax.axis_index("wall") // 2

    @pl.when(chip == 2)
    def _():
        def column(j, carry):
            state = [[chip_ref[0, r, i, j] for i in range(size)] for r in range(2)]
            state = block_vector(entry(beside_ref), state)
            state = block_vector(entry(chip_ref, 1), state)
            for r in range(2):
                for i in range(size):
                    out_ref[r, i, j] = chip_ref[2, r, i, j] + state[r][i]
            return carry

        lax.fori_loop(0, size, column, 0)

    @pl.when(chip != 2)
    def _():
        out_ref[...] = jnp.zeros_like(out_ref)


def local_kernel(
    columns, spans, rows, pivot_ref, lower_ref, upper_ref, scale_ref, *refs
):
    arrived = refs[:spans]
    source_ref, keep_ref, send_ref, driving_ref, sweep_ref = refs[spans:]
    size = pivot_ref.shape[2]
    points = pivot_ref.shape[4]
    half = points // 2
    groups = spans // rows
    at = lax.axis_index("span")
    scale = jnp.max(scale_ref[...])
    for m in range(spans):
        y = (m // groups) ^ (at // groups)
        for t in range(columns // groups):
            c = t * groups + ((m % groups) ^ (at % groups)) if groups > 1 else t
            driving_ref[y, c] = arrived[m][t] * scale
    core = lax.axis_index("wall") % 2

    def solve(part, carry):
        span = pl.ds(part * half, half)
        states = None
        for y in range(rows):
            drivings = [load_vector(driving_ref.at[y, c], size, span) for c in range(columns)]
            news = block_vectors(entry(pivot_ref, y, rows=span), drivings)
            for c in range(columns):
                store_vector(source_ref.at[y, c], news[c], span)
            if states is not None:
                moved = block_vectors(entry(lower_ref, y, rows=span), states)
                news = [minus(new, move) for new, move in zip(news, moved)]
            states = news
            for c in range(columns):
                store_vector(sweep_ref.at[y, c], states[c])
        for y in range(rows - 2, -1, -1):
            moved = block_vectors(entry(upper_ref, y, rows=span), states)
            states = [
                minus(load_vector(sweep_ref.at[y, c], size), moved[c]) for c in range(columns)
            ]

        def put(ref):
            for c in range(columns):
                ref[0, c] = sweep_ref[rows - 1, c]
                store_vector(ref.at[1, c], states[c])

        @pl.when(part == core)
        def _():
            put(keep_ref)

        @pl.when(part != core)
        def _():
            put(send_ref)

        return carry

    lax.fori_loop(0, 2, solve, 0)


def pair_kernel(
    columns, chips, pair_ref, keep_ref, other_ref, chip_ref, inner_ref, send_ref, both_ref
):
    core = lax.axis_index("wall") % 2
    low = lax.axis_index("wall") // 2 < chips // 2
    size = pair_ref.shape[3]
    both_ref[core] = keep_ref[...]
    both_ref[1 - core] = other_ref[...]

    def column(c, carry):
        first = load_vector(both_ref.at[0, 0, c], size)
        forth = plus(
            load_vector(both_ref.at[1, 0, c], size), block_vector(entry(pair_ref, 1, 0), first)
        )
        entering = plus(
            load_vector(both_ref.at[1, 1, c], size), block_vector(entry(pair_ref, 1, 2), first)
        )
        back = plus(
            load_vector(both_ref.at[0, 1, c], size),
            block_vector(entry(pair_ref, 0, 1), entering),
        )
        store_vector(inner_ref.at[0, c], first)
        store_vector(inner_ref.at[1, c], entering)
        store_vector(chip_ref.at[0, c], forth)
        store_vector(chip_ref.at[1, c], back)

        @pl.when(low)
        def _():
            store_vector(send_ref.at[c], forth)

        @pl.when(jnp.logical_not(low))
        def _():
            store_vector(send_ref.at[c], back)

        return carry

    lax.fori_loop(0, columns, column, 0)


def halves_kernel(
    columns, matrices_ref, beside_ref, chip_ref, came_ref, out_ref
):
    size = beside_ref.shape[1]
    chip = lax.axis_index("wall") // 2

    @pl.when(chip == 1)
    def _():
        def column(c, carry):
            moved = block_vector(entry(matrices_ref, 0), load_vector(came_ref.at[c], size))
            store_vector(out_ref.at[c], plus(load_vector(chip_ref.at[0, c], size), moved))
            return carry

        lax.fori_loop(0, columns, column, 0)

    @pl.when(chip == 2)
    def _():
        def column(c, carry):
            forth = load_vector(chip_ref.at[0, c], size)
            moved = plus(load_vector(came_ref.at[c], size), block_vector(entry(beside_ref), forth))
            moved = block_vector(entry(matrices_ref, 1), moved)
            store_vector(out_ref.at[c], plus(load_vector(chip_ref.at[1, c], size), moved))
            return carry

        lax.fori_loop(0, columns, column, 0)

    @pl.when((chip == 0) | (chip == 3))
    def _():
        out_ref[...] = jnp.zeros_like(out_ref)


def middle_kernel(
    columns,
    matrices_ref,
    beside_ref,
    upper_ref,
    chip_ref,
    first_ref,
    mine_ref,
    came_ref,
    edge_ref,
    out_ref,
):
    size = beside_ref.shape[1]
    chip = lax.axis_index("wall") // 2

    @pl.when(chip == 1)
    def _():
        def column(c, carry):
            answer = plus(
                load_vector(came_ref.at[c], size),
                block_vector(entry(upper_ref), load_vector(mine_ref.at[c], size)),
            )
            store_vector(edge_ref.at[1, c], answer)
            onward = plus(
                load_vector(chip_ref.at[1, c], size), block_vector(entry(matrices_ref, 1), answer)
            )
            entering = load_vector(first_ref.at[c], size)
            store_vector(edge_ref.at[0, c], entering)
            store_vector(
                out_ref.at[c], plus(onward, block_vector(entry(matrices_ref, 2), entering))
            )
            return carry

        lax.fori_loop(0, columns, column, 0)

    @pl.when(chip == 2)
    def _():
        def column(c, carry):
            entering = load_vector(came_ref.at[c], size)
            store_vector(edge_ref.at[0, c], entering)
            onward = plus(
                load_vector(chip_ref.at[0, c], size),
                block_vector(entry(matrices_ref, 0), entering),
            )
            store_vector(out_ref.at[c], onward)
            store_vector(
                edge_ref.at[1, c],
                plus(
                    load_vector(first_ref.at[c], size), block_vector(entry(beside_ref), onward)
                ),
            )
            return carry

        lax.fori_loop(0, columns, column, 0)

    @pl.when((chip == 0) | (chip == 3))
    def _():
        edge_ref[...] = jnp.zeros_like(edge_ref)
        out_ref[...] = jnp.zeros_like(out_ref)


def split_kernel(
    columns, outer, pair_ref, joint_ref, inner_ref, edge_ref, *refs
):
    came_ref = refs[0] if outer else None
    keep_ref, send_ref, entry_ref = refs[-3:]
    core, chip = lax.axis_index("wall") % 2, lax.axis_index("wall") // 2
    size = pair_ref.shape[3]
    entry_ref[...] = edge_ref[...]
    if outer:

        @pl.when(chip == 0)
        def _():
            entry_ref[1] = came_ref[...]

        @pl.when(chip == 3)
        def _():
            entry_ref[0] = came_ref[...]

    def column(c, carry):
        sweep = load_vector(entry_ref.at[0, c], size)
        upper_sweep = plus(
            load_vector(inner_ref.at[0, c], size), block_vector(entry(pair_ref, 0, 0), sweep)
        )
        middle = plus(
            load_vector(inner_ref.at[1, c], size), block_vector(entry(joint_ref), sweep)
        )
        answer = load_vector(entry_ref.at[1, c], size)
        lower_answer = plus(middle, block_vector(entry(pair_ref, 1, 1), answer))

        def put(lower_target, upper_target):
            store_vector(lower_target.at[0, c], sweep)
            store_vector(lower_target.at[1, c], lower_answer)
            store_vector(upper_target.at[0, c], upper_sweep)
            store_vector(upper_target.at[1, c], answer)

        @pl.when(core == 0)
        def _():
            put(keep_ref, send_ref)

        @pl.when(core == 1)
        def _():
            put(send_ref, keep_ref)

        return carry

    lax.fori_loop(0, columns, column, 0)


def answer_kernel(
    columns, first, rows, lower_ref, upper_ref, source_ref, keep_ref, other_ref, *refs
):
    sweep_ref, edge_ref = refs[-2:]
    last = first is not None
    earlier = refs[: len(refs) - 5] if last else ()
    out_ref, made_ref, done = refs[len(earlier) : -2] if last else (None, refs[0], None)
    core = lax.axis_index("wall") % 2
    size = lower_ref.shape[2]
    points = lower_ref.shape[4]
    half = points // 2
    edge_ref[core] = keep_ref[...]
    edge_ref[1 - core] = other_ref[...]

    def copies(place, part, ref):
        return [
            pltpu.make_async_copy(
                ref.at[part, r, i],
                out_ref.at[
                    r,
                    i,
                    pl.ds(place * columns, columns),
                    pl.ds(part * half * rows, half * rows),
                ],
                done.at[place, part, r, i],
            )
            for r in range(2)
            for i in range(size)
        ]

    started = [
        copy
        for place, ref in enumerate(earlier)
        for part in range(2)
        for copy in copies(place, part, ref)
    ]
    for copy in started:
        copy.start()

    def run(part, carry):
        span = pl.ds(part * half, half)
        states = [load_vector(edge_ref.at[part, 0, c], size) for c in range(columns)]
        for y in range(rows):
            moved = block_vectors(entry(lower_ref, y, rows=span), states)
            states = [
                minus(load_vector(source_ref.at[y, c], size, span), moved[c])
                for c in range(columns)
            ]
            for c in range(columns):
                store_vector(sweep_ref.at[y, c], states[c])
        states = [load_vector(edge_ref.at[part, 1, c], size) for c in range(columns)]
        for y in range(rows - 1, -1, -1):
            moved = block_vectors(entry(upper_ref, y, rows=span), states)
            states = [
                minus(load_vector(sweep_ref.at[y, c], size), moved[c]) for c in range(columns)
            ]
            place = pl.ds(y, half, stride=rows)
            for c in range(columns):
                for r in range(2):
                    for i in range(size):
                        made_ref[part, r, i, c, place] = states[c][r][i]
        if last:
            for copy in copies(len(earlier), part, made_ref):
                copy.start()
        return carry

    lax.fori_loop(0, 2, run, 0)
    if last:
        started += copies(len(earlier), 0, made_ref) + copies(len(earlier), 1, made_ref)
        for copy in started:
            copy.wait()


def affine(matrix, vector, offset):
    left_re, left_im = matrix[0][None], matrix[1][None]
    right_re, right_im = vector[:, 0, None], vector[:, 1, None]
    real = jnp.sum(left_re * right_re - left_im * right_im, axis=2)
    imag = jnp.sum(left_re * right_im + left_im * right_re, axis=2)
    return offset + jnp.stack([real, imag], axis=1)


def local(forcing, span_factor, pivot_inverse, step_lower, step_upper):
    parts, fields, columns, points, rows, width = forcing.shape
    spans, walls = lax.axis_size("span"), lax.axis_size("wall")
    chips = walls // 2
    half = points // 2

    flat = (points * rows, width)
    forcing = forcing.reshape(forcing.shape[:3] + flat)
    pivot_inverse = pivot_inverse.reshape(pivot_inverse.shape[:3] + flat)
    step_lower = step_lower.reshape(step_lower.shape[:3] + flat)
    step_upper = step_upper.reshape(step_upper.shape[:3] + flat)

    def swap(array, distance, axis, name):
        count = spans if axis == "span" else walls
        with jax.named_scope(name):
            return lax.ppermute(array, axis, [(i, i ^ distance) for i in range(count)])

    def gate(array, *earlier):
        return lax.optimization_barrier((array,) + earlier)[0]

    groups = spans // rows
    block = (columns // groups * 2 * fields + 1, points, width)
    mark = f32(8, width)
    repacked, *sent = call(
        functools.partial(repack_kernel, rows, groups),
        [mark] + [jax.ShapeDtypeStruct(block, jnp.bfloat16)] * spans,
        micros=2.0,
        in_specs=[vmem()],
    )(forcing)
    sent = [sent[0]] + [
        swap(sent[m], m, "span", f"forcing{m}") for m in range(1, spans)
    ]

    kept = jnp.bfloat16 if half % 16 == 0 else jnp.float32
    moved_shape = jax.ShapeDtypeStruct((rows, 2, fields, fields, points, width), kept)
    plane = (half, width)
    summary = f32(3, 2, fields, fields, *plane)
    def reorder(matrix, after):
        return call(
            functools.partial(reorder_kernel, rows),
            moved_shape,
            micros=2.0,
            in_specs=[vmem(), anywhere()],
        )(matrix, after)

    lowers, uppers = reorder(step_lower, repacked), reorder(step_upper, repacked)
    summarized, keep, send = call(
        functools.partial(summary_kernel, rows),
        [mark] + [summary] * 2,
            micros=6.0,
        scratch=[pltpu.VMEM((rows, 2, 2, fields) + plane, jnp.float32)],
        in_specs=[vmem()] * 2,
    )(lowers, uppers)
    kernel = call(
        functools.partial(table_kernel, points),
        jax.ShapeDtypeStruct((fields, 4 * spans * points, 2 * spans * points), jnp.bfloat16),
        micros=2.0,
        in_specs=[vmem(), anywhere()],
    )(span_factor, summarized)
    scale, *outs = call(
        functools.partial(filter_kernel, spans, len(CHUNKS)),
        [f32(8, 128)]
        + [f32(columns // len(CHUNKS) // groups, 2, fields, points, width)]
        * (spans * len(CHUNKS)),
        micros=1.0,
        in_specs=[vmem()] * (1 + spans),
    )(kernel, *sent)
    drivings = []
    for number in range(len(CHUNKS)):
        own = outs[number * spans : (number + 1) * spans]
        drivings.append(
            [own[0]]
            + [
                swap(
                    own[m].astype(jnp.float16), m, "span", f"chunk{number}_driving{m}"
                ).astype(jnp.float32)
                for m in range(1, spans)
            ]
        )

    pivots = reorder(pivot_inverse, scale)
    other = swap(gate(send, scale), 1, "wall", "matrices_core")
    pair, chip_matrices, joint = call(
        pair_matrices_kernel,
        [
            f32(2, *summary.shape),
            summary,
            f32(2, fields, fields, *plane),
        ],
            micros=1.4,
        in_specs=[anywhere()] + [vmem()] * 2,
    )(scale, keep, other)
    tree = chips == 4
    outward = [(i, i ^ 2) for i in range(walls)]
    inward = [(0, 1), (1, 0), (2, 4), (4, 2), (3, 5), (5, 3), (6, 7), (7, 6)]
    if tree:
        with jax.named_scope("matrices_outward"):
            beside = lax.ppermute(chip_matrices[2], "wall", outward)

    began, finished = [], []
    for number, chosen in enumerate(CHUNKS):
        count = len(chosen)
        vectors = f32(2, count, 2, fields, *plane)
        single = f32(count, 2, fields, *plane)
        size = 2 * fields * count * half * width
        taken = drivings[number]
        source, keep, send = call(
            functools.partial(local_kernel, count, spans, rows),
            [f32(rows, count, 2, fields, points, width), vectors, vectors],
            micros=1.4 * count,
            scratch=[
                pltpu.VMEM((rows, count, 2, fields, points, width), jnp.float32),
                pltpu.VMEM((rows, count, 2, fields) + plane, jnp.float32),
            ],
            in_specs=[vmem()] * (4 + len(taken)),
        )(pivots, lowers, uppers, scale, *taken)
        other = swap(send, 1, "wall", f"chunk{number}_core")
        chip, inner, outgoing = call(
            functools.partial(pair_kernel, count, chips),
            [vectors, vectors, single],
            micros=0.25 * count,
            scratch=[pltpu.VMEM((2,) + vectors.shape, jnp.float32)],
            in_specs=[vmem()] * 3,
        )(pair, keep, other)
        began.append((source, chip, inner, outgoing))

    if tree:
        upper_half = call(
            upper_half_kernel,
            f32(2, fields, fields, *plane),
            micros=0.7,
            in_specs=[vmem()] * 2,
        )(chip_matrices, beside)
        with jax.named_scope("matrices_inward"):
            upper_half = lax.ppermute(upper_half, "wall", inward)
    for number, chosen in enumerate(CHUNKS):
        count = len(chosen)
        vectors = f32(2, count, 2, fields, *plane)
        single = f32(count, 2, fields, *plane)
        source, chip, inner, outgoing = began[number]
        extra = ()
        if tree:
            with jax.named_scope(f"chunk{number}_to_middle"):
                came = lax.ppermute(outgoing, "wall", outward)
            mine = call(
                functools.partial(halves_kernel, count),
                single,
                micros=0.2 * count,
                in_specs=[vmem()] * 4,
            )(chip_matrices, beside, chip, came)
            with jax.named_scope(f"chunk{number}_middle"):
                across = lax.ppermute(mine, "wall", inward)
            edge, outgoing = call(
                functools.partial(middle_kernel, count),
                [vectors, single],
                micros=0.2 * count,
                in_specs=[vmem()] * 7,
            )(chip_matrices, beside, upper_half, chip, came, mine, across)
            with jax.named_scope(f"chunk{number}_to_ends"):
                extra = (lax.ppermute(outgoing, "wall", outward),)
        else:
            sweep = jnp.zeros(single.shape, jnp.float32)
            answer = jnp.zeros(single.shape, jnp.float32)
            upward = [(i, i + 2) for i in range(walls - 2)]
            downward = [(i + 2, i) for i in range(walls - 2)]
            for _ in range(chips - 1):
                sweep = lax.ppermute(affine(chip_matrices[0], sweep, chip[0]), "wall", upward)
            offset = affine(chip_matrices[2], sweep, chip[1])
            for _ in range(chips - 1):
                answer = lax.ppermute(affine(chip_matrices[1], answer, offset), "wall", downward)
            edge = jnp.stack([sweep, answer])
        keep, send = call(
            functools.partial(split_kernel, count, tree),
            [vectors, vectors],
            micros=0.25 * count,
            scratch=[pltpu.VMEM(vectors.shape, jnp.float32)],
            in_specs=[vmem()] * (4 + len(extra)),
        )(pair, joint, inner, edge, *extra)
        other = swap(send, 1, "wall", f"chunk{number}_apart")
        final = number == len(CHUNKS) - 1
        made = (2, 2, fields, count, half * rows, width)
        scratch = [
            pltpu.VMEM((rows, count, 2, fields) + plane, jnp.float32),
            pltpu.VMEM((2,) + vectors.shape, jnp.float32),
        ]
        if final:
            scratch = [
                pltpu.VMEM(made, jnp.float32),
                pltpu.SemaphoreType.DMA((len(CHUNKS), 2, 2, fields)),
            ] + scratch
        finished.append(
            call(
                functools.partial(answer_kernel, count, chosen[0] if final else None, rows),
                f32(2, fields, columns, *flat) if final else f32(*made),
                micros=1.5 * count,
                scratch=scratch,
                in_specs=[vmem()] * (5 + (len(finished) if final else 0)),
                out_specs=anywhere() if final else vmem(),
            )(lowers, uppers, source, keep, other, *(finished if final else ()))
        )
    out = finished[-1]
    return out.reshape(2, fields, columns, points, rows, width)


def solution(mesh):
    placed = (
        P(None, None, None, "span", "wall", None),
        P(),
        P(None, None, None, "span", "wall", None),
        P(None, None, None, "span", "wall", None),
        P(None, None, None, "span", "wall", None),
    )
    return jax.shard_map(
        local,
        mesh=mesh,
        in_specs=placed,
        out_specs=P(None, None, None, "span", "wall", None),
        check_vma=False,
    )
```

```python
import functools
import math

import jax
import jax.numpy as jnp
from jax import lax
from jax.experimental import pallas as pl
from jax.experimental.pallas import tpu as pltpu
from jax.sharding import PartitionSpec as P

exact_mode = lax.Precision.HIGHEST
VMEM_LIMIT = 24 * 1024 * 1024
BYTES_PER_MICRO = 3_600_000
CHUNKS = ((0, 1), (2, 3))


def call(kernel, out_shape, scratch=(), micros=1.0, limit=VMEM_LIMIT, **options):
    plain = kernel.func if isinstance(kernel, functools.partial) else kernel
    return pl.pallas_call(
        kernel,
        name=plain.__name__,
        out_shape=out_shape,
        scratch_shapes=scratch,
        compiler_params=pltpu.CompilerParams(vmem_limit_bytes=limit),
        cost_estimate=pl.CostEstimate(
            flops=0, bytes_accessed=int(micros * BYTES_PER_MICRO), transcendentals=0
        ),
        **options,
    )


def vmem():
    return pl.BlockSpec(memory_space=pltpu.VMEM)


def anywhere():
    return pl.BlockSpec(memory_space=pl.ANY)


def f32(*shape):
    return jax.ShapeDtypeStruct(shape, jnp.float32)


def block_vectors(matrix, vectors):
    size = len(vectors[0][0])
    out = [([], []) for _ in vectors]
    for i in range(size):
        totals = [None] * len(vectors)
        for j in range(size):
            a, b = matrix(0, i, j), matrix(1, i, j)
            for place, vector in enumerate(vectors):
                c, d = vector[0][j], vector[1][j]
                term = (a * c - b * d, a * d + b * c)
                if j > 0:
                    term = (totals[place][0] + term[0], totals[place][1] + term[1])
                totals[place] = term
        for place, total in enumerate(totals):
            out[place][0].append(total[0])
            out[place][1].append(total[1])
    return out


def block_vector(matrix, vector):
    return block_vectors(matrix, [vector])[0]


def plus(left, right):
    return [[a + b for a, b in zip(x, y)] for x, y in zip(left, right)]


def minus(left, right):
    return [[a - b for a, b in zip(x, y)] for x, y in zip(left, right)]


def negative(vector):
    return [[-a for a in x] for x in vector]


def load_vector(ref, size, *where):
    return [[ref[(r, i) + where] for i in range(size)] for r in range(2)]


def store_vector(ref, vector, *where):
    for r in range(2):
        for i, plane in enumerate(vector[r]):
            ref[(r, i) + where] = plane


def entry(ref, *lead, rows=slice(None)):
    return lambda r, i, j: ref[lead + (r, i, j, rows)].astype(jnp.float32)


def reorder_matrix(points, rows, turn=0):
    size = points * rows
    to = lax.broadcasted_iota(jnp.int32, (size, size), 0)
    of = lax.broadcasted_iota(jnp.int32, (size, size), 1)
    wanted = (to % points) * rows + ((to // points) ^ turn)
    return jnp.where(of == wanted, 1.0, 0.0).astype(jnp.bfloat16)


def repack_kernel(rows, groups, forcing_ref, mark_ref, *out_refs):
    fields, columns = forcing_ref.shape[1:3]
    points = forcing_ref.shape[3] // rows
    each = columns // groups
    at = lax.axis_index("span")
    order = reorder_matrix(points, rows, at // groups)
    peak = jnp.zeros((points * rows, 256), jnp.float32)
    for r in range(2):
        for i in range(fields):
            for b in range(groups):
                for t in range(0, each, 2):
                    chosen = [
                        (t + side) * groups + (b ^ (at % groups)) if groups > 1 else t + side
                        for side in range(2)
                    ]
                    pair = jnp.concatenate(
                        [forcing_ref[r, i, column] for column in chosen], axis=1
                    )
                    moved = jnp.dot(order, pair, preferred_element_type=jnp.float32)
                    peak = jnp.maximum(peak, jnp.abs(moved))
                    moved = moved.astype(jnp.bfloat16)
                    for side in range(2):
                        plane = ((t + side) * 2 + r) * fields + i
                        for j in range(rows):
                            out_refs[j * groups + b][plane] = moved[
                                j * points : (j + 1) * points, side * 128 : (side + 1) * 128
                            ]
    peak = jnp.max(peak)
    mark_ref[...] = jnp.zeros_like(mark_ref)
    for ref in out_refs:
        ref[each * 2 * fields] = jnp.full(ref.shape[1:], peak, jnp.float32).astype(jnp.bfloat16)


def table_kernel(own, factor_ref, after_ref, out_ref):
    fields, count = factor_ref.shape[1:]
    at = lax.axis_index("span")
    scale = 2.0 * math.pi / count

    def grid(shape, dimension):
        return lax.broadcasted_iota(jnp.int32, shape, dimension)

    def point(slot):
        return (at ^ (slot // own)) * own + slot % own

    wide = (count, 2 * count)
    column = grid(wide, 1)
    source = point((column // (2 * own)) * own + column % own)
    turn = (column // own) % 2 * (count // 4)
    steps = (grid(wide, 0) * source + count - turn) % count
    angle = steps.astype(jnp.float32) * scale
    right = jnp.concatenate([jnp.cos(angle), jnp.sin(angle)], axis=0)
    square = (count, count)
    angle = (point(grid(square, 0)) * grid(square, 1) % count).astype(jnp.float32) * scale
    cosine, sine = jnp.cos(angle) / count, jnp.sin(angle) / count
    for i in range(fields):
        factor_re, factor_im = factor_ref[0, i : i + 1], factor_ref[1, i : i + 1]
        left_re = factor_re * cosine - factor_im * sine
        left_im = factor_re * sine + factor_im * cosine
        for part, left in enumerate(([left_re, left_im], [left_im, -left_re])):
            whole = jnp.dot(
                jnp.concatenate(left, axis=1),
                right,
                precision=exact_mode,
                preferred_element_type=jnp.float32,
            )
            high = whole.astype(jnp.bfloat16)
            low = (whole - high.astype(jnp.float32)).astype(jnp.bfloat16)
            for m in range(count // own):
                base = (4 * m + part) * own
                rows = slice(m * own, (m + 1) * own)
                out_ref[i, base : base + own] = high[rows]
                out_ref[i, base + 2 * own : base + 3 * own] = low[rows]


def filter_kernel(sources, chunks, kernel_ref, *refs):
    arrived, scale_ref, outs = refs[:1] + refs[1:sources][::-1], refs[sources], refs[sources + 1 :]
    each, fields, points = outs[0].shape[0] * chunks, outs[0].shape[2], outs[0].shape[3]
    last = arrived[0].shape[0] - 1
    peak = arrived[0][last].astype(jnp.float32)
    for m in range(1, sources):
        peak = jnp.maximum(peak, arrived[m][last].astype(jnp.float32))
    peak = jnp.maximum(jnp.max(peak), 1e-30)
    scale = 2048.0 / jnp.full((8, 128), peak, jnp.float32)
    scale_ref[...] = jnp.full((8, 128), peak, jnp.float32) / 2048.0
    scale = jnp.max(scale)
    for i in range(fields):
        right = jnp.concatenate(
            [
                jnp.concatenate(
                    [
                        arrived[m][(t * 2 + r) * fields + i]
                        for m in range(sources)
                        for r in range(2)
                    ],
                    axis=0,
                )
                for t in range(each)
            ],
            axis=1,
        )
        both = jnp.dot(kernel_ref[i], right, preferred_element_type=jnp.float32)
        for m in range(sources):
            base = m * 4 * points
            total = (
                both[base : base + 2 * points] + both[base + 2 * points : base + 4 * points]
            ) * scale
            for t in range(each):
                for r in range(2):
                    outs[t * chunks // each * sources + m][t % (each // chunks), r, i] = total[
                        r * points : (r + 1) * points, t * 128 : (t + 1) * 128
                    ]


def reorder_kernel(rows, in_ref, after_ref, out_ref):
    size = in_ref.shape[1]
    points = in_ref.shape[3] // rows
    order = reorder_matrix(points, rows)

    def move(index, carry):
        r, i = index // size, index % size
        wide = jnp.concatenate([in_ref[r, i, j] for j in range(size)], axis=1)
        moved = jnp.dot(order, wide, preferred_element_type=jnp.float32).astype(out_ref.dtype)
        for j in range(size):
            for y in range(rows):
                out_ref[y, r, i, j] = moved[
                    y * points : (y + 1) * points, j * 128 : (j + 1) * 128
                ]
        return carry

    lax.fori_loop(0, 2 * size, move, 0)


def summary_kernel(rows, lower_ref, upper_ref, mark_ref, keep_ref, send_ref, held_ref):
    size = lower_ref.shape[2]
    half = lower_ref.shape[4] // 2
    core = lax.axis_index("wall") % 2
    mark_ref[...] = jnp.zeros_like(mark_ref)

    def summarize(part, chosen):
        span = pl.ds(part * half, half)

        def column(ref, y):
            return [
                [
                    [-ref[y, r, i, j, span].astype(jnp.float32) for i in range(size)]
                    for r in range(2)
                ]
                for j in chosen
            ]

        def store(which, vectors):
            @pl.when(part == core)
            def _():
                for j, vector in zip(chosen, vectors):
                    for r in range(2):
                        for i in range(size):
                            keep_ref[which, r, i, j] = vector[r][i]

            @pl.when(part != core)
            def _():
                for j, vector in zip(chosen, vectors):
                    for r in range(2):
                        for i in range(size):
                            send_ref[which, r, i, j] = vector[r][i]

        states = column(lower_ref, 0)
        for place, state in enumerate(states):
            store_vector(held_ref.at[0, place], state)
        for y in range(1, rows):
            moved = block_vectors(entry(lower_ref, y, rows=span), states)
            states = [negative(move) for move in moved]
            for place, state in enumerate(states):
                store_vector(held_ref.at[y, place], state)
        store(0, states)
        for y in range(rows - 2, -1, -1):
            moved = block_vectors(entry(upper_ref, y, rows=span), states)
            states = [
                minus(load_vector(held_ref.at[y, place], size), move)
                for place, move in enumerate(moved)
            ]
        store(2, states)
        states = column(upper_ref, rows - 1)
        for y in range(rows - 2, -1, -1):
            moved = block_vectors(entry(upper_ref, y, rows=span), states)
            states = [negative(move) for move in moved]
        store(1, states)

    def half_of(part, carry):
        def pair(step, carry):
            summarize(part, [2 * step, 2 * step + 1])
            return carry

        lax.fori_loop(0, size // 2, pair, 0)
        if size % 2:
            summarize(part, [size - 1])
        return carry

    lax.fori_loop(0, 2, half_of, 0)


def pair_matrices_kernel(
    after_ref, keep_ref, other_ref, mark_ref, pair_ref, chip_ref, joint_ref
):
    mark_ref[...] = jnp.zeros_like(mark_ref)
    core = lax.axis_index("wall") % 2
    size = keep_ref.shape[2]
    for which in range(3):
        for r in range(2):
            for i in range(size):
                for j in range(size):
                    pair_ref[core, which, r, i, j] = keep_ref[which, r, i, j]
                    pair_ref[1 - core, which, r, i, j] = other_ref[which, r, i, j]

    def column(j, carry):
        def read(*lead):
            return [[pair_ref[lead + (r, i, j)] for i in range(size)] for r in range(2)]

        def write(ref, vector, *lead):
            for r in range(2):
                for i in range(size):
                    ref[lead + (r, i, j)] = vector[r][i]

        through = read(0, 0)
        write(chip_ref, block_vector(entry(pair_ref, 1, 0), through), 0)
        write(chip_ref, block_vector(entry(pair_ref, 0, 1), read(1, 1)), 1)
        joint = block_vector(entry(pair_ref, 1, 2), through)
        write(joint_ref, joint)
        write(chip_ref, plus(read(0, 2), block_vector(entry(pair_ref, 0, 1), joint)), 2)
        return carry

    lax.fori_loop(0, size, column, 0)


def upper_half_kernel(*refs):
    chip_ref, beside_ref, out_ref = refs[-3:]
    size = chip_ref.shape[2]

    chip = lax.axis_index("wall") // 2

    @pl.when(chip == 2)
    def _():
        def column(j, carry):
            state = [[chip_ref[0, r, i, j] for i in range(size)] for r in range(2)]
            state = block_vector(entry(beside_ref), state)
            state = block_vector(entry(chip_ref, 1), state)
            for r in range(2):
                for i in range(size):
                    out_ref[r, i, j] = chip_ref[2, r, i, j] + state[r][i]
            return carry

        lax.fori_loop(0, size, column, 0)

    @pl.when(chip != 2)
    def _():
        out_ref[...] = jnp.zeros_like(out_ref)


def local_kernel(
    columns, spans, rows, pivot_ref, lower_ref, upper_ref, scale_ref, *refs
):
    arrived = refs[:spans]
    source_ref, keep_ref, send_ref, driving_ref, sweep_ref = refs[spans:]
    size = pivot_ref.shape[2]
    points = pivot_ref.shape[4]
    half = points // 2
    groups = spans // rows
    at = lax.axis_index("span")
    scale = jnp.max(scale_ref[...])
    for m in range(spans):
        y = (m // groups) ^ (at // groups)
        for t in range(columns // groups):
            c = t * groups + ((m % groups) ^ (at % groups)) if groups > 1 else t
            driving_ref[y, c] = arrived[m][t] * scale
    core = lax.axis_index("wall") % 2

    def solve(part, carry):
        span = pl.ds(part * half, half)
        states = None
        for y in range(rows):
            drivings = [load_vector(driving_ref.at[y, c], size, span) for c in range(columns)]
            news = block_vectors(entry(pivot_ref, y, rows=span), drivings)
            for c in range(columns):
                store_vector(source_ref.at[y, c], news[c], span)
            if states is not None:
                moved = block_vectors(entry(lower_ref, y, rows=span), states)
                news = [minus(new, move) for new, move in zip(news, moved)]
            states = news
            for c in range(columns):
                store_vector(sweep_ref.at[y, c], states[c])
        for y in range(rows - 2, -1, -1):
            moved = block_vectors(entry(upper_ref, y, rows=span), states)
            states = [
                minus(load_vector(sweep_ref.at[y, c], size), moved[c]) for c in range(columns)
            ]

        def put(ref):
            for c in range(columns):
                ref[0, c] = sweep_ref[rows - 1, c]
                store_vector(ref.at[1, c], states[c])

        @pl.when(part == core)
        def _():
            put(keep_ref)

        @pl.when(part != core)
        def _():
            put(send_ref)

        return carry

    lax.fori_loop(0, 2, solve, 0)


def pair_kernel(
    columns, chips, pair_ref, keep_ref, other_ref, chip_ref, inner_ref, send_ref, both_ref
):
    core = lax.axis_index("wall") % 2
    low = lax.axis_index("wall") // 2 < chips // 2
    size = pair_ref.shape[3]
    both_ref[core] = keep_ref[...]
    both_ref[1 - core] = other_ref[...]

    def column(c, carry):
        first = load_vector(both_ref.at[0, 0, c], size)
        forth = plus(
            load_vector(both_ref.at[1, 0, c], size), block_vector(entry(pair_ref, 1, 0), first)
        )
        entering = plus(
            load_vector(both_ref.at[1, 1, c], size), block_vector(entry(pair_ref, 1, 2), first)
        )
        back = plus(
            load_vector(both_ref.at[0, 1, c], size),
            block_vector(entry(pair_ref, 0, 1), entering),
        )
        store_vector(inner_ref.at[0, c], first)
        store_vector(inner_ref.at[1, c], entering)
        store_vector(chip_ref.at[0, c], forth)
        store_vector(chip_ref.at[1, c], back)

        @pl.when(low)
        def _():
            store_vector(send_ref.at[c], forth)

        @pl.when(jnp.logical_not(low))
        def _():
            store_vector(send_ref.at[c], back)

        return carry

    lax.fori_loop(0, columns, column, 0)


def halves_kernel(
    columns, matrices_ref, beside_ref, chip_ref, came_ref, out_ref
):
    size = beside_ref.shape[1]
    chip = lax.axis_index("wall") // 2

    @pl.when(chip == 1)
    def _():
        def column(c, carry):
            moved = block_vector(entry(matrices_ref, 0), load_vector(came_ref.at[c], size))
            store_vector(out_ref.at[c], plus(load_vector(chip_ref.at[0, c], size), moved))
            return carry

        lax.fori_loop(0, columns, column, 0)

    @pl.when(chip == 2)
    def _():
        def column(c, carry):
            forth = load_vector(chip_ref.at[0, c], size)
            moved = plus(load_vector(came_ref.at[c], size), block_vector(entry(beside_ref), forth))
            moved = block_vector(entry(matrices_ref, 1), moved)
            store_vector(out_ref.at[c], plus(load_vector(chip_ref.at[1, c], size), moved))
            return carry

        lax.fori_loop(0, columns, column, 0)

    @pl.when((chip == 0) | (chip == 3))
    def _():
        out_ref[...] = jnp.zeros_like(out_ref)


def middle_kernel(
    columns,
    matrices_ref,
    beside_ref,
    upper_ref,
    chip_ref,
    first_ref,
    mine_ref,
    came_ref,
    edge_ref,
    out_ref,
):
    size = beside_ref.shape[1]
    chip = lax.axis_index("wall") // 2

    @pl.when(chip == 1)
    def _():
        def column(c, carry):
            answer = plus(
                load_vector(came_ref.at[c], size),
                block_vector(entry(upper_ref), load_vector(mine_ref.at[c], size)),
            )
            store_vector(edge_ref.at[1, c], answer)
            onward = plus(
                load_vector(chip_ref.at[1, c], size), block_vector(entry(matrices_ref, 1), answer)
            )
            entering = load_vector(first_ref.at[c], size)
            store_vector(edge_ref.at[0, c], entering)
            store_vector(
                out_ref.at[c], plus(onward, block_vector(entry(matrices_ref, 2), entering))
            )
            return carry

        lax.fori_loop(0, columns, column, 0)

    @pl.when(chip == 2)
    def _():
        def column(c, carry):
            entering = load_vector(came_ref.at[c], size)
            store_vector(edge_ref.at[0, c], entering)
            onward = plus(
                load_vector(chip_ref.at[0, c], size),
                block_vector(entry(matrices_ref, 0), entering),
            )
            store_vector(out_ref.at[c], onward)
            store_vector(
                edge_ref.at[1, c],
                plus(
                    load_vector(first_ref.at[c], size), block_vector(entry(beside_ref), onward)
                ),
            )
            return carry

        lax.fori_loop(0, columns, column, 0)

    @pl.when((chip == 0) | (chip == 3))
    def _():
        edge_ref[...] = jnp.zeros_like(edge_ref)
        out_ref[...] = jnp.zeros_like(out_ref)


def split_kernel(
    columns, outer, pair_ref, joint_ref, inner_ref, edge_ref, *refs
):
    came_ref = refs[0] if outer else None
    keep_ref, send_ref, entry_ref = refs[-3:]
    core, chip = lax.axis_index("wall") % 2, lax.axis_index("wall") // 2
    size = pair_ref.shape[3]
    entry_ref[...] = edge_ref[...]
    if outer:

        @pl.when(chip == 0)
        def _():
            entry_ref[1] = came_ref[...]

        @pl.when(chip == 3)
        def _():
            entry_ref[0] = came_ref[...]

    def column(c, carry):
        sweep = load_vector(entry_ref.at[0, c], size)
        upper_sweep = plus(
            load_vector(inner_ref.at[0, c], size), block_vector(entry(pair_ref, 0, 0), sweep)
        )
        middle = plus(
            load_vector(inner_ref.at[1, c], size), block_vector(entry(joint_ref), sweep)
        )
        answer = load_vector(entry_ref.at[1, c], size)
        lower_answer = plus(middle, block_vector(entry(pair_ref, 1, 1), answer))

        def put(lower_target, upper_target):
            store_vector(lower_target.at[0, c], sweep)
            store_vector(lower_target.at[1, c], lower_answer)
            store_vector(upper_target.at[0, c], upper_sweep)
            store_vector(upper_target.at[1, c], answer)

        @pl.when(core == 0)
        def _():
            put(keep_ref, send_ref)

        @pl.when(core == 1)
        def _():
            put(send_ref, keep_ref)

        return carry

    lax.fori_loop(0, columns, column, 0)


def answer_kernel(
    columns, first, rows, lower_ref, upper_ref, source_ref, keep_ref, other_ref, *refs
):
    sweep_ref, edge_ref = refs[-2:]
    last = first is not None
    earlier = refs[: len(refs) - 5] if last else ()
    out_ref, made_ref, done = refs[len(earlier) : -2] if last else (None, refs[0], None)
    core = lax.axis_index("wall") % 2
    size = lower_ref.shape[2]
    points = lower_ref.shape[4]
    half = points // 2
    edge_ref[core] = keep_ref[...]
    edge_ref[1 - core] = other_ref[...]

    def copies(place, part, ref):
        return [
            pltpu.make_async_copy(
                ref.at[part, r, i],
                out_ref.at[
                    r,
                    i,
                    pl.ds(place * columns, columns),
                    pl.ds(part * half * rows, half * rows),
                ],
                done.at[place, part, r, i],
            )
            for r in range(2)
            for i in range(size)
        ]

    started = [
        copy
        for place, ref in enumerate(earlier)
        for part in range(2)
        for copy in copies(place, part, ref)
    ]
    for copy in started:
        copy.start()

    def run(part, carry):
        span = pl.ds(part * half, half)
        states = [load_vector(edge_ref.at[part, 0, c], size) for c in range(columns)]
        for y in range(rows):
            moved = block_vectors(entry(lower_ref, y, rows=span), states)
            states = [
                minus(load_vector(source_ref.at[y, c], size, span), moved[c])
                for c in range(columns)
            ]
            for c in range(columns):
                store_vector(sweep_ref.at[y, c], states[c])
        states = [load_vector(edge_ref.at[part, 1, c], size) for c in range(columns)]
        for y in range(rows - 1, -1, -1):
            moved = block_vectors(entry(upper_ref, y, rows=span), states)
            states = [
                minus(load_vector(sweep_ref.at[y, c], size), moved[c]) for c in range(columns)
            ]
            place = pl.ds(y, half, stride=rows)
            for c in range(columns):
                for r in range(2):
                    for i in range(size):
                        made_ref[part, r, i, c, place] = states[c][r][i]
        if last:
            for copy in copies(len(earlier), part, made_ref):
                copy.start()
        return carry

    lax.fori_loop(0, 2, run, 0)
    if last:
        started += copies(len(earlier), 0, made_ref) + copies(len(earlier), 1, made_ref)
        for copy in started:
            copy.wait()


def affine(matrix, vector, offset):
    left_re, left_im = matrix[0][None], matrix[1][None]
    right_re, right_im = vector[:, 0, None], vector[:, 1, None]
    real = jnp.sum(left_re * right_re - left_im * right_im, axis=2)
    imag = jnp.sum(left_re * right_im + left_im * right_re, axis=2)
    return offset + jnp.stack([real, imag], axis=1)


def local(forcing, span_factor, pivot_inverse, step_lower, step_upper):
    parts, fields, columns, points, rows, width = forcing.shape
    spans, walls = lax.axis_size("span"), lax.axis_size("wall")
    chips = walls // 2
    half = points // 2

    flat = (points * rows, width)
    forcing = forcing.reshape(forcing.shape[:3] + flat)
    pivot_inverse = pivot_inverse.reshape(pivot_inverse.shape[:3] + flat)
    step_lower = step_lower.reshape(step_lower.shape[:3] + flat)
    step_upper = step_upper.reshape(step_upper.shape[:3] + flat)

    def swap(array, distance, axis, name):
        count = spans if axis == "span" else walls
        with jax.named_scope(name):
            return lax.ppermute(array, axis, [(i, i ^ distance) for i in range(count)])

    def gate(array, *earlier):
        return lax.optimization_barrier((array,) + earlier)[0]

    groups = spans // rows
    block = (columns // groups * 2 * fields + 1, points, width)
    mark = f32(8, width)
    repacked, *sent = call(
        functools.partial(repack_kernel, rows, groups),
        [mark] + [jax.ShapeDtypeStruct(block, jnp.bfloat16)] * spans,
        micros=2.0,
        in_specs=[vmem()],
    )(forcing)
    back = [swap(sent[m], m, "span", f"forcing{m}") for m in range(spans - 1, 0, -1)]
    sent = [sent[0]] + back[::-1]

    kept = jnp.bfloat16 if half % 16 == 0 else jnp.float32
    moved_shape = jax.ShapeDtypeStruct((rows, 2, fields, fields, points, width), kept)
    plane = (half, width)
    summary = f32(3, 2, fields, fields, *plane)
    def reorder(matrix, after):
        return call(
            functools.partial(reorder_kernel, rows),
            moved_shape,
            micros=2.0,
            in_specs=[vmem(), anywhere()],
        )(matrix, after)

    lowers, uppers = reorder(step_lower, repacked), reorder(step_upper, repacked)
    summarized, keep, send = call(
        functools.partial(summary_kernel, rows),
        [mark] + [summary] * 2,
            micros=6.0,
        scratch=[pltpu.VMEM((rows, 2, 2, fields) + plane, jnp.float32)],
        in_specs=[vmem()] * 2,
    )(lowers, uppers)
    kernel = call(
        functools.partial(table_kernel, points),
        jax.ShapeDtypeStruct((fields, 4 * spans * points, 2 * spans * points), jnp.bfloat16),
        micros=2.0,
        in_specs=[vmem(), anywhere()],
    )(span_factor, summarized)
    scale, *outs = call(
        functools.partial(filter_kernel, spans, len(CHUNKS)),
        [f32(8, 128)]
        + [f32(columns // len(CHUNKS) // groups, 2, fields, points, width)]
        * (spans * len(CHUNKS)),
        micros=1.0,
        in_specs=[vmem()] * (1 + spans),
    )(kernel, sent[0], *sent[:0:-1])
    pivots = reorder(pivot_inverse, scale)
    other = swap(gate(send, scale), 1, "wall", "matrices_core")
    paired, pair, chip_matrices, joint = call(
        pair_matrices_kernel,
        [
            mark,
            f32(2, *summary.shape),
            summary,
            f32(2, fields, fields, *plane),
        ],
            micros=1.4,
        in_specs=[anywhere()] + [vmem()] * 2,
    )(scale, keep, other)
    drivings = []
    for number in range(len(CHUNKS)):
        own = outs[number * spans : (number + 1) * spans]
        narrow = [array.astype(jnp.float16) for array in own]
        if number > 0:
            narrow = [gate(array, paired) for array in narrow]
        drivings.append(
            [own[0]]
            + [
                swap(narrow[m], m, "span", f"chunk{number}_driving{m}").astype(jnp.float32)
                for m in range(1, spans)
            ]
        )

    tree = chips == 4
    outward = [(i, i ^ 2) for i in range(walls)]
    inward = [(0, 1), (1, 0), (2, 4), (4, 2), (3, 5), (5, 3), (6, 7), (7, 6)]
    if tree:
        with jax.named_scope("matrices_outward"):
            beside = lax.ppermute(chip_matrices[2], "wall", outward)

    began, finished = [], []
    for number, chosen in enumerate(CHUNKS):
        count = len(chosen)
        vectors = f32(2, count, 2, fields, *plane)
        single = f32(count, 2, fields, *plane)
        size = 2 * fields * count * half * width
        taken = drivings[number]
        source, keep, send = call(
            functools.partial(local_kernel, count, spans, rows),
            [f32(rows, count, 2, fields, points, width), vectors, vectors],
            micros=1.4 * count,
            scratch=[
                pltpu.VMEM((rows, count, 2, fields, points, width), jnp.float32),
                pltpu.VMEM((rows, count, 2, fields) + plane, jnp.float32),
            ],
            in_specs=[vmem()] * (4 + len(taken)),
        )(pivots, lowers, uppers, scale, *taken)
        other = swap(send, 1, "wall", f"chunk{number}_core")
        chip, inner, outgoing = call(
            functools.partial(pair_kernel, count, chips),
            [vectors, vectors, single],
            micros=0.25 * count,
            scratch=[pltpu.VMEM((2,) + vectors.shape, jnp.float32)],
            in_specs=[vmem()] * 3,
        )(pair, keep, other)
        began.append((source, chip, inner, outgoing))

    if tree:
        upper_half = call(
            upper_half_kernel,
            f32(2, fields, fields, *plane),
            micros=0.7,
            in_specs=[vmem()] * 2,
        )(chip_matrices, beside)
        with jax.named_scope("matrices_inward"):
            upper_half = lax.ppermute(upper_half, "wall", inward)
    for number, chosen in enumerate(CHUNKS):
        count = len(chosen)
        vectors = f32(2, count, 2, fields, *plane)
        single = f32(count, 2, fields, *plane)
        source, chip, inner, outgoing = began[number]
        extra = ()
        if tree:
            with jax.named_scope(f"chunk{number}_to_middle"):
                came = lax.ppermute(outgoing, "wall", outward)
            mine = call(
                functools.partial(halves_kernel, count),
                single,
                micros=0.2 * count,
                in_specs=[vmem()] * 4,
            )(chip_matrices, beside, chip, came)
            with jax.named_scope(f"chunk{number}_middle"):
                across = lax.ppermute(mine, "wall", inward)
            edge, outgoing = call(
                functools.partial(middle_kernel, count),
                [vectors, single],
                micros=0.2 * count,
                in_specs=[vmem()] * 7,
            )(chip_matrices, beside, upper_half, chip, came, mine, across)
            with jax.named_scope(f"chunk{number}_to_ends"):
                extra = (lax.ppermute(outgoing, "wall", outward),)
        else:
            sweep = jnp.zeros(single.shape, jnp.float32)
            answer = jnp.zeros(single.shape, jnp.float32)
            upward = [(i, i + 2) for i in range(walls - 2)]
            downward = [(i + 2, i) for i in range(walls - 2)]
            for _ in range(chips - 1):
                sweep = lax.ppermute(affine(chip_matrices[0], sweep, chip[0]), "wall", upward)
            offset = affine(chip_matrices[2], sweep, chip[1])
            for _ in range(chips - 1):
                answer = lax.ppermute(affine(chip_matrices[1], answer, offset), "wall", downward)
            edge = jnp.stack([sweep, answer])
        keep, send = call(
            functools.partial(split_kernel, count, tree),
            [vectors, vectors],
            micros=0.25 * count,
            scratch=[pltpu.VMEM(vectors.shape, jnp.float32)],
            in_specs=[vmem()] * (4 + len(extra)),
        )(pair, joint, inner, edge, *extra)
        other = swap(send, 1, "wall", f"chunk{number}_apart")
        final = number == len(CHUNKS) - 1
        made = (2, 2, fields, count, half * rows, width)
        scratch = [
            pltpu.VMEM((rows, count, 2, fields) + plane, jnp.float32),
            pltpu.VMEM((2,) + vectors.shape, jnp.float32),
        ]
        if final:
            scratch = [
                pltpu.VMEM(made, jnp.float32),
                pltpu.SemaphoreType.DMA((len(CHUNKS), 2, 2, fields)),
            ] + scratch
        finished.append(
            call(
                functools.partial(answer_kernel, count, chosen[0] if final else None, rows),
                f32(2, fields, columns, *flat) if final else f32(*made),
                micros=1.5 * count,
                scratch=scratch,
                in_specs=[vmem()] * (5 + (len(finished) if final else 0)),
                out_specs=anywhere() if final else vmem(),
            )(lowers, uppers, source, keep, other, *(finished if final else ()))
        )
    out = finished[-1]
    return out.reshape(2, fields, columns, points, rows, width)


def solution(mesh):
    placed = (
        P(None, None, None, "span", "wall", None),
        P(),
        P(None, None, None, "span", "wall", None),
        P(None, None, None, "span", "wall", None),
        P(None, None, None, "span", "wall", None),
    )
    return jax.shard_map(
        local,
        mesh=mesh,
        in_specs=placed,
        out_specs=P(None, None, None, "span", "wall", None),
        check_vma=False,
    )
```

```python
import functools
import math

import jax
import jax.numpy as jnp
from jax import lax
from jax.experimental import pallas as pl
from jax.experimental.pallas import tpu as pltpu
from jax.sharding import PartitionSpec as P

exact_mode = lax.Precision.HIGHEST
VMEM_LIMIT = 24 * 1024 * 1024
BYTES_PER_MICRO = 3_600_000
CHUNKS = ((0, 1), (2, 3))


def call(kernel, out_shape, scratch=(), micros=1.0, limit=VMEM_LIMIT, **options):
    plain = kernel.func if isinstance(kernel, functools.partial) else kernel
    return pl.pallas_call(
        kernel,
        name=plain.__name__,
        out_shape=out_shape,
        scratch_shapes=scratch,
        compiler_params=pltpu.CompilerParams(vmem_limit_bytes=limit),
        cost_estimate=pl.CostEstimate(
            flops=0, bytes_accessed=int(micros * BYTES_PER_MICRO), transcendentals=0
        ),
        **options,
    )


def vmem():
    return pl.BlockSpec(memory_space=pltpu.VMEM)


def anywhere():
    return pl.BlockSpec(memory_space=pl.ANY)


def f32(*shape):
    return jax.ShapeDtypeStruct(shape, jnp.float32)


def block_vectors(matrix, vectors):
    size = len(vectors[0][0])
    out = [([], []) for _ in vectors]
    for i in range(size):
        totals = [None] * len(vectors)
        for j in range(size):
            a, b = matrix(0, i, j), matrix(1, i, j)
            for place, vector in enumerate(vectors):
                c, d = vector[0][j], vector[1][j]
                term = (a * c - b * d, a * d + b * c)
                if j > 0:
                    term = (totals[place][0] + term[0], totals[place][1] + term[1])
                totals[place] = term
        for place, total in enumerate(totals):
            out[place][0].append(total[0])
            out[place][1].append(total[1])
    return out


def block_vector(matrix, vector):
    return block_vectors(matrix, [vector])[0]


def plus(left, right):
    return [[a + b for a, b in zip(x, y)] for x, y in zip(left, right)]


def minus(left, right):
    return [[a - b for a, b in zip(x, y)] for x, y in zip(left, right)]


def negative(vector):
    return [[-a for a in x] for x in vector]


def load_vector(ref, size, *where):
    return [[ref[(r, i) + where] for i in range(size)] for r in range(2)]


def store_vector(ref, vector, *where):
    for r in range(2):
        for i, plane in enumerate(vector[r]):
            ref[(r, i) + where] = plane


def entry(ref, *lead, rows=slice(None)):
    return lambda r, i, j: ref[lead + (r, i, j, rows)].astype(jnp.float32)


def reorder_matrix(points, rows, turn=0):
    size = points * rows
    to = lax.broadcasted_iota(jnp.int32, (size, size), 0)
    of = lax.broadcasted_iota(jnp.int32, (size, size), 1)
    wanted = (to % points) * rows + ((to // points) ^ turn)
    return jnp.where(of == wanted, 1.0, 0.0).astype(jnp.bfloat16)


def repack_kernel(rows, groups, forcing_ref, mark_ref, *out_refs):
    fields, columns = forcing_ref.shape[1:3]
    points = forcing_ref.shape[3] // rows
    each = columns // groups
    at = lax.axis_index("span")
    order = reorder_matrix(points, rows, at // groups)
    peak = jnp.zeros((points * rows, 256), jnp.float32)
    for r in range(2):
        for i in range(fields):
            for b in range(groups):
                for t in range(0, each, 2):
                    chosen = [
                        (t + side) * groups + (b ^ (at % groups)) if groups > 1 else t + side
                        for side in range(2)
                    ]
                    pair = jnp.concatenate(
                        [forcing_ref[r, i, column] for column in chosen], axis=1
                    )
                    moved = jnp.dot(order, pair, preferred_element_type=jnp.float32)
                    peak = jnp.maximum(peak, jnp.abs(moved))
                    moved = moved.astype(jnp.bfloat16)
                    for side in range(2):
                        plane = ((t + side) * 2 + r) * fields + i
                        for j in range(rows):
                            out_refs[j * groups + b][plane] = moved[
                                j * points : (j + 1) * points, side * 128 : (side + 1) * 128
                            ]
    peak = jnp.max(peak)
    mark_ref[...] = jnp.zeros_like(mark_ref)
    for ref in out_refs:
        ref[each * 2 * fields] = jnp.full(ref.shape[1:], peak, jnp.float32).astype(jnp.bfloat16)


def table_kernel(own, factor_ref, after_ref, out_ref):
    fields, count = factor_ref.shape[1:]
    at = lax.axis_index("span")
    scale = 2.0 * math.pi / count

    def grid(shape, dimension):
        return lax.broadcasted_iota(jnp.int32, shape, dimension)

    def point(slot):
        return (at ^ (slot // own)) * own + slot % own

    wide = (count, 2 * count)
    column = grid(wide, 1)
    source = point((column // (2 * own)) * own + column % own)
    turn = (column // own) % 2 * (count // 4)
    steps = (grid(wide, 0) * source + count - turn) % count
    angle = steps.astype(jnp.float32) * scale
    right = jnp.concatenate([jnp.cos(angle), jnp.sin(angle)], axis=0)
    square = (count, count)
    angle = (point(grid(square, 0)) * grid(square, 1) % count).astype(jnp.float32) * scale
    cosine, sine = jnp.cos(angle) / count, jnp.sin(angle) / count
    for i in range(fields):
        factor_re, factor_im = factor_ref[0, i : i + 1], factor_ref[1, i : i + 1]
        left_re = factor_re * cosine - factor_im * sine
        left_im = factor_re * sine + factor_im * cosine
        for part, left in enumerate(([left_re, left_im], [left_im, -left_re])):
            whole = jnp.dot(
                jnp.concatenate(left, axis=1),
                right,
                precision=exact_mode,
                preferred_element_type=jnp.float32,
            )
            high = whole.astype(jnp.bfloat16)
            low = (whole - high.astype(jnp.float32)).astype(jnp.bfloat16)
            for m in range(count // own):
                base = (4 * m + part) * own
                rows = slice(m * own, (m + 1) * own)
                out_ref[i, base : base + own] = high[rows]
                out_ref[i, base + 2 * own : base + 3 * own] = low[rows]


def filter_kernel(sources, chunks, kernel_ref, *refs):
    arrived, scale_ref, outs = refs[:1] + refs[1:sources][::-1], refs[sources], refs[sources + 1 :]
    each, fields, points = outs[0].shape[0] * chunks, outs[0].shape[2], outs[0].shape[3]
    last = arrived[0].shape[0] - 1
    peak = arrived[0][last].astype(jnp.float32)
    for m in range(1, sources):
        peak = jnp.maximum(peak, arrived[m][last].astype(jnp.float32))
    peak = jnp.maximum(jnp.max(peak), 1e-30)
    scale = 2048.0 / jnp.full((8, 128), peak, jnp.float32)
    scale_ref[...] = jnp.full((8, 128), peak, jnp.float32) / 2048.0
    scale = jnp.max(scale)
    for i in range(fields):
        right = jnp.concatenate(
            [
                jnp.concatenate(
                    [
                        arrived[m][(t * 2 + r) * fields + i]
                        for m in range(sources)
                        for r in range(2)
                    ],
                    axis=0,
                )
                for t in range(each)
            ],
            axis=1,
        )
        both = jnp.dot(kernel_ref[i], right, preferred_element_type=jnp.float32)
        for m in range(sources):
            base = m * 4 * points
            total = (
                both[base : base + 2 * points] + both[base + 2 * points : base + 4 * points]
            ) * scale
            for t in range(each):
                for r in range(2):
                    outs[t * chunks // each * sources + m][t % (each // chunks), r, i] = total[
                        r * points : (r + 1) * points, t * 128 : (t + 1) * 128
                    ]


def reorder_kernel(rows, in_ref, after_ref, out_ref):
    size = in_ref.shape[1]
    points = in_ref.shape[3] // rows
    order = reorder_matrix(points, rows)

    def move(index, carry):
        r, i = index // size, index % size
        wide = jnp.concatenate([in_ref[r, i, j] for j in range(size)], axis=1)
        moved = jnp.dot(order, wide, preferred_element_type=jnp.float32).astype(out_ref.dtype)
        for j in range(size):
            for y in range(rows):
                out_ref[y, r, i, j] = moved[
                    y * points : (y + 1) * points, j * 128 : (j + 1) * 128
                ]
        return carry

    lax.fori_loop(0, 2 * size, move, 0)


def summary_kernel(rows, lower_ref, upper_ref, mark_ref, keep_ref, send_ref, held_ref):
    size = lower_ref.shape[2]
    half = lower_ref.shape[4] // 2
    core = lax.axis_index("wall") % 2
    mark_ref[...] = jnp.zeros_like(mark_ref)

    def summarize(part, chosen):
        span = pl.ds(part * half, half)

        def column(ref, y):
            return [
                [
                    [-ref[y, r, i, j, span].astype(jnp.float32) for i in range(size)]
                    for r in range(2)
                ]
                for j in chosen
            ]

        def store(which, vectors):
            @pl.when(part == core)
            def _():
                for j, vector in zip(chosen, vectors):
                    for r in range(2):
                        for i in range(size):
                            keep_ref[which, r, i, j] = vector[r][i]

            @pl.when(part != core)
            def _():
                for j, vector in zip(chosen, vectors):
                    for r in range(2):
                        for i in range(size):
                            send_ref[which, r, i, j] = vector[r][i]

        states = column(lower_ref, 0)
        for place, state in enumerate(states):
            store_vector(held_ref.at[0, place], state)
        for y in range(1, rows):
            moved = block_vectors(entry(lower_ref, y, rows=span), states)
            states = [negative(move) for move in moved]
            for place, state in enumerate(states):
                store_vector(held_ref.at[y, place], state)
        store(0, states)
        for y in range(rows - 2, -1, -1):
            moved = block_vectors(entry(upper_ref, y, rows=span), states)
            states = [
                minus(load_vector(held_ref.at[y, place], size), move)
                for place, move in enumerate(moved)
            ]
        store(2, states)
        states = column(upper_ref, rows - 1)
        for y in range(rows - 2, -1, -1):
            moved = block_vectors(entry(upper_ref, y, rows=span), states)
            states = [negative(move) for move in moved]
        store(1, states)

    def half_of(part, carry):
        def pair(step, carry):
            summarize(part, [2 * step, 2 * step + 1])
            return carry

        lax.fori_loop(0, size // 2, pair, 0)
        if size % 2:
            summarize(part, [size - 1])
        return carry

    lax.fori_loop(0, 2, half_of, 0)


def pair_matrices_kernel(
    after_ref, keep_ref, other_ref, mark_ref, pair_ref, chip_ref, joint_ref
):
    mark_ref[...] = jnp.zeros_like(mark_ref)
    core = lax.axis_index("wall") % 2
    size = keep_ref.shape[2]
    for which in range(3):
        for r in range(2):
            for i in range(size):
                for j in range(size):
                    pair_ref[core, which, r, i, j] = keep_ref[which, r, i, j]
                    pair_ref[1 - core, which, r, i, j] = other_ref[which, r, i, j]

    def column(j, carry):
        def read(*lead):
            return [[pair_ref[lead + (r, i, j)] for i in range(size)] for r in range(2)]

        def write(ref, vector, *lead):
            for r in range(2):
                for i in range(size):
                    ref[lead + (r, i, j)] = vector[r][i]

        through = read(0, 0)
        write(chip_ref, block_vector(entry(pair_ref, 1, 0), through), 0)
        write(chip_ref, block_vector(entry(pair_ref, 0, 1), read(1, 1)), 1)
        joint = block_vector(entry(pair_ref, 1, 2), through)
        write(joint_ref, joint)
        write(chip_ref, plus(read(0, 2), block_vector(entry(pair_ref, 0, 1), joint)), 2)
        return carry

    lax.fori_loop(0, size, column, 0)


def upper_half_kernel(*refs):
    chip_ref, beside_ref, out_ref = refs[-3:]
    size = chip_ref.shape[2]

    chip = lax.axis_index("wall") // 2

    @pl.when(chip == 2)
    def _():
        def column(j, carry):
            state = [[chip_ref[0, r, i, j] for i in range(size)] for r in range(2)]
            state = block_vector(entry(beside_ref), state)
            state = block_vector(entry(chip_ref, 1), state)
            for r in range(2):
                for i in range(size):
                    out_ref[r, i, j] = chip_ref[2, r, i, j] + state[r][i]
            return carry

        lax.fori_loop(0, size, column, 0)

    @pl.when(chip != 2)
    def _():
        out_ref[...] = jnp.zeros_like(out_ref)


def local_kernel(
    columns, spans, rows, pivot_ref, lower_ref, upper_ref, scale_ref, *refs
):
    arrived = refs[:spans]
    source_ref, keep_ref, send_ref, sweep_ref = refs[spans:]
    size = pivot_ref.shape[2]
    points = pivot_ref.shape[4]
    half = points // 2
    groups = spans // rows
    each = columns // groups
    at = lax.axis_index("span")
    scale = jnp.max(scale_ref[...])
    core = lax.axis_index("wall") % 2

    def solve(part, carry):
        span = pl.ds(part * half, half)
        for m in range(spans):
            y = (m // groups) ^ (at // groups)
            drivings = [
                [[plane * scale for plane in side] for side in load_vector(ref, size, span)]
                for ref in (arrived[m].at[t] for t in range(each))
            ]
            for t, new in enumerate(block_vectors(entry(pivot_ref, y, rows=span), drivings)):
                c = t * groups + ((m % groups) ^ (at % groups)) if groups > 1 else t
                store_vector(source_ref.at[y, c], new, span)
        states = None
        for y in range(rows):
            news = [load_vector(source_ref.at[y, c], size, span) for c in range(columns)]
            if states is not None:
                moved = block_vectors(entry(lower_ref, y, rows=span), states)
                news = [minus(new, move) for new, move in zip(news, moved)]
            states = news
            for c in range(columns):
                store_vector(sweep_ref.at[y, c], states[c])
        for y in range(rows - 2, -1, -1):
            moved = block_vectors(entry(upper_ref, y, rows=span), states)
            states = [
                minus(load_vector(sweep_ref.at[y, c], size), moved[c]) for c in range(columns)
            ]

        def put(ref):
            for c in range(columns):
                ref[0, c] = sweep_ref[rows - 1, c]
                store_vector(ref.at[1, c], states[c])

        @pl.when(part == core)
        def _():
            put(keep_ref)

        @pl.when(part != core)
        def _():
            put(send_ref)

        return carry

    lax.fori_loop(0, 2, solve, 0)


def pair_kernel(
    columns, chips, pair_ref, keep_ref, other_ref, chip_ref, inner_ref, send_ref, both_ref
):
    core = lax.axis_index("wall") % 2
    low = lax.axis_index("wall") // 2 < chips // 2
    size = pair_ref.shape[3]
    both_ref[core] = keep_ref[...]
    both_ref[1 - core] = other_ref[...]

    def column(c, carry):
        first = load_vector(both_ref.at[0, 0, c], size)
        forth = plus(
            load_vector(both_ref.at[1, 0, c], size), block_vector(entry(pair_ref, 1, 0), first)
        )
        entering = plus(
            load_vector(both_ref.at[1, 1, c], size), block_vector(entry(pair_ref, 1, 2), first)
        )
        back = plus(
            load_vector(both_ref.at[0, 1, c], size),
            block_vector(entry(pair_ref, 0, 1), entering),
        )
        store_vector(inner_ref.at[0, c], first)
        store_vector(inner_ref.at[1, c], entering)
        store_vector(chip_ref.at[0, c], forth)
        store_vector(chip_ref.at[1, c], back)

        @pl.when(low)
        def _():
            store_vector(send_ref.at[c], forth)

        @pl.when(jnp.logical_not(low))
        def _():
            store_vector(send_ref.at[c], back)

        return carry

    lax.fori_loop(0, columns, column, 0)


def halves_kernel(
    columns, matrices_ref, beside_ref, chip_ref, came_ref, out_ref
):
    size = beside_ref.shape[1]
    chip = lax.axis_index("wall") // 2

    @pl.when(chip == 1)
    def _():
        def column(c, carry):
            moved = block_vector(entry(matrices_ref, 0), load_vector(came_ref.at[c], size))
            store_vector(out_ref.at[c], plus(load_vector(chip_ref.at[0, c], size), moved))
            return carry

        lax.fori_loop(0, columns, column, 0)

    @pl.when(chip == 2)
    def _():
        def column(c, carry):
            forth = load_vector(chip_ref.at[0, c], size)
            moved = plus(load_vector(came_ref.at[c], size), block_vector(entry(beside_ref), forth))
            moved = block_vector(entry(matrices_ref, 1), moved)
            store_vector(out_ref.at[c], plus(load_vector(chip_ref.at[1, c], size), moved))
            return carry

        lax.fori_loop(0, columns, column, 0)

    @pl.when((chip == 0) | (chip == 3))
    def _():
        out_ref[...] = jnp.zeros_like(out_ref)


def middle_kernel(
    columns,
    matrices_ref,
    beside_ref,
    upper_ref,
    chip_ref,
    first_ref,
    mine_ref,
    came_ref,
    edge_ref,
    out_ref,
):
    size = beside_ref.shape[1]
    chip = lax.axis_index("wall") // 2

    @pl.when(chip == 1)
    def _():
        def column(c, carry):
            answer = plus(
                load_vector(came_ref.at[c], size),
                block_vector(entry(upper_ref), load_vector(mine_ref.at[c], size)),
            )
            store_vector(edge_ref.at[1, c], answer)
            onward = plus(
                load_vector(chip_ref.at[1, c], size), block_vector(entry(matrices_ref, 1), answer)
            )
            entering = load_vector(first_ref.at[c], size)
            store_vector(edge_ref.at[0, c], entering)
            store_vector(
                out_ref.at[c], plus(onward, block_vector(entry(matrices_ref, 2), entering))
            )
            return carry

        lax.fori_loop(0, columns, column, 0)

    @pl.when(chip == 2)
    def _():
        def column(c, carry):
            entering = load_vector(came_ref.at[c], size)
            store_vector(edge_ref.at[0, c], entering)
            onward = plus(
                load_vector(chip_ref.at[0, c], size),
                block_vector(entry(matrices_ref, 0), entering),
            )
            store_vector(out_ref.at[c], onward)
            store_vector(
                edge_ref.at[1, c],
                plus(
                    load_vector(first_ref.at[c], size), block_vector(entry(beside_ref), onward)
                ),
            )
            return carry

        lax.fori_loop(0, columns, column, 0)

    @pl.when((chip == 0) | (chip == 3))
    def _():
        edge_ref[...] = jnp.zeros_like(edge_ref)
        out_ref[...] = jnp.zeros_like(out_ref)


def split_kernel(
    columns, outer, pair_ref, joint_ref, inner_ref, edge_ref, *refs
):
    came_ref = refs[0] if outer else None
    keep_ref, send_ref, entry_ref = refs[-3:]
    core, chip = lax.axis_index("wall") % 2, lax.axis_index("wall") // 2
    size = pair_ref.shape[3]
    entry_ref[...] = edge_ref[...]
    if outer:

        @pl.when(chip == 0)
        def _():
            entry_ref[1] = came_ref[...]

        @pl.when(chip == 3)
        def _():
            entry_ref[0] = came_ref[...]

    def column(c, carry):
        sweep = load_vector(entry_ref.at[0, c], size)
        upper_sweep = plus(
            load_vector(inner_ref.at[0, c], size), block_vector(entry(pair_ref, 0, 0), sweep)
        )
        middle = plus(
            load_vector(inner_ref.at[1, c], size), block_vector(entry(joint_ref), sweep)
        )
        answer = load_vector(entry_ref.at[1, c], size)
        lower_answer = plus(middle, block_vector(entry(pair_ref, 1, 1), answer))

        def put(lower_target, upper_target):
            store_vector(lower_target.at[0, c], sweep)
            store_vector(lower_target.at[1, c], lower_answer)
            store_vector(upper_target.at[0, c], upper_sweep)
            store_vector(upper_target.at[1, c], answer)

        @pl.when(core == 0)
        def _():
            put(keep_ref, send_ref)

        @pl.when(core == 1)
        def _():
            put(send_ref, keep_ref)

        return carry

    lax.fori_loop(0, columns, column, 0)


def answer_kernel(
    columns, first, rows, lower_ref, upper_ref, source_ref, keep_ref, other_ref, *refs
):
    sweep_ref, edge_ref = refs[-2:]
    last = first is not None
    earlier = refs[: len(refs) - 5] if last else ()
    out_ref, made_ref, done = refs[len(earlier) : -2] if last else (None, refs[0], None)
    core = lax.axis_index("wall") % 2
    size = lower_ref.shape[2]
    points = lower_ref.shape[4]
    half = points // 2
    edge_ref[core] = keep_ref[...]
    edge_ref[1 - core] = other_ref[...]

    def copies(place, part, ref):
        return [
            pltpu.make_async_copy(
                ref.at[part, r, i],
                out_ref.at[
                    r,
                    i,
                    pl.ds(place * columns, columns),
                    pl.ds(part * half * rows, half * rows),
                ],
                done.at[place, part, r, i],
            )
            for r in range(2)
            for i in range(size)
        ]

    started = [
        copy
        for place, ref in enumerate(earlier)
        for part in range(2)
        for copy in copies(place, part, ref)
    ]
    for copy in started:
        copy.start()

    def run(part, carry):
        span = pl.ds(part * half, half)
        states = [load_vector(edge_ref.at[part, 0, c], size) for c in range(columns)]
        for y in range(rows):
            moved = block_vectors(entry(lower_ref, y, rows=span), states)
            states = [
                minus(load_vector(source_ref.at[y, c], size, span), moved[c])
                for c in range(columns)
            ]
            for c in range(columns):
                store_vector(sweep_ref.at[y, c], states[c])
        states = [load_vector(edge_ref.at[part, 1, c], size) for c in range(columns)]
        for y in range(rows - 1, -1, -1):
            moved = block_vectors(entry(upper_ref, y, rows=span), states)
            states = [
                minus(load_vector(sweep_ref.at[y, c], size), moved[c]) for c in range(columns)
            ]
            place = pl.ds(y, half, stride=rows)
            for c in range(columns):
                for r in range(2):
                    for i in range(size):
                        made_ref[part, r, i, c, place] = states[c][r][i]
        if last:
            for copy in copies(len(earlier), part, made_ref):
                copy.start()
        return carry

    lax.fori_loop(0, 2, run, 0)
    if last:
        started += copies(len(earlier), 0, made_ref) + copies(len(earlier), 1, made_ref)
        for copy in started:
            copy.wait()


def affine(matrix, vector, offset):
    left_re, left_im = matrix[0][None], matrix[1][None]
    right_re, right_im = vector[:, 0, None], vector[:, 1, None]
    real = jnp.sum(left_re * right_re - left_im * right_im, axis=2)
    imag = jnp.sum(left_re * right_im + left_im * right_re, axis=2)
    return offset + jnp.stack([real, imag], axis=1)


def local(forcing, span_factor, pivot_inverse, step_lower, step_upper):
    parts, fields, columns, points, rows, width = forcing.shape
    spans, walls = lax.axis_size("span"), lax.axis_size("wall")
    chips = walls // 2
    half = points // 2

    flat = (points * rows, width)
    forcing = forcing.reshape(forcing.shape[:3] + flat)
    pivot_inverse = pivot_inverse.reshape(pivot_inverse.shape[:3] + flat)
    step_lower = step_lower.reshape(step_lower.shape[:3] + flat)
    step_upper = step_upper.reshape(step_upper.shape[:3] + flat)

    def swap(array, distance, axis, name):
        count = spans if axis == "span" else walls
        with jax.named_scope(name):
            return lax.ppermute(array, axis, [(i, i ^ distance) for i in range(count)])

    def gate(array, *earlier):
        return lax.optimization_barrier((array,) + earlier)[0]

    groups = spans // rows
    block = (columns // groups * 2 * fields + 1, points, width)
    mark = f32(8, width)
    repacked, *sent = call(
        functools.partial(repack_kernel, rows, groups),
        [mark] + [jax.ShapeDtypeStruct(block, jnp.bfloat16)] * spans,
        micros=2.0,
        in_specs=[vmem()],
    )(forcing)
    back = [swap(sent[m], m, "span", f"forcing{m}") for m in range(spans - 1, 0, -1)]
    sent = [sent[0]] + back[::-1]

    kept = jnp.bfloat16 if half % 16 == 0 else jnp.float32
    moved_shape = jax.ShapeDtypeStruct((rows, 2, fields, fields, points, width), kept)
    plane = (half, width)
    summary = f32(3, 2, fields, fields, *plane)
    def reorder(matrix, after):
        return call(
            functools.partial(reorder_kernel, rows),
            moved_shape,
            micros=2.0,
            in_specs=[vmem(), anywhere()],
        )(matrix, after)

    lowers, uppers = reorder(step_lower, repacked), reorder(step_upper, repacked)
    summarized, keep, send = call(
        functools.partial(summary_kernel, rows),
        [mark] + [summary] * 2,
            micros=6.0,
        scratch=[pltpu.VMEM((rows, 2, 2, fields) + plane, jnp.float32)],
        in_specs=[vmem()] * 2,
    )(lowers, uppers)
    kernel = call(
        functools.partial(table_kernel, points),
        jax.ShapeDtypeStruct((fields, 4 * spans * points, 2 * spans * points), jnp.bfloat16),
        micros=2.0,
        in_specs=[vmem(), anywhere()],
    )(span_factor, summarized)
    scale, *outs = call(
        functools.partial(filter_kernel, spans, len(CHUNKS)),
        [f32(8, 128)]
        + [f32(columns // len(CHUNKS) // groups, 2, fields, points, width)]
        * (spans * len(CHUNKS)),
        micros=1.0,
        in_specs=[vmem()] * (1 + spans),
    )(kernel, sent[0], *sent[:0:-1])
    pivots = reorder(pivot_inverse, scale)
    other = swap(gate(send, scale), 1, "wall", "matrices_core")
    paired, pair, chip_matrices, joint = call(
        pair_matrices_kernel,
        [
            mark,
            f32(2, *summary.shape),
            summary,
            f32(2, fields, fields, *plane),
        ],
            micros=1.4,
        in_specs=[anywhere()] + [vmem()] * 2,
    )(scale, keep, other)
    drivings = []
    for number in range(len(CHUNKS)):
        own = outs[number * spans : (number + 1) * spans]
        narrow = [array.astype(jnp.float16) for array in own]
        if number > 0:
            narrow = [gate(array, paired) for array in narrow]
        drivings.append(
            [own[0]]
            + [
                swap(narrow[m], m, "span", f"chunk{number}_driving{m}").astype(jnp.float32)
                for m in range(1, spans)
            ]
        )

    tree = chips == 4
    outward = [(i, i ^ 2) for i in range(walls)]
    inward = [(0, 1), (1, 0), (2, 4), (4, 2), (3, 5), (5, 3), (6, 7), (7, 6)]
    if tree:
        with jax.named_scope("matrices_outward"):
            beside = lax.ppermute(chip_matrices[2], "wall", outward)

    began, finished = [], []
    for number, chosen in enumerate(CHUNKS):
        count = len(chosen)
        vectors = f32(2, count, 2, fields, *plane)
        single = f32(count, 2, fields, *plane)
        size = 2 * fields * count * half * width
        taken = drivings[number]
        source, keep, send = call(
            functools.partial(local_kernel, count, spans, rows),
            [f32(rows, count, 2, fields, points, width), vectors, vectors],
            micros=1.4 * count,
            scratch=[
                pltpu.VMEM((rows, count, 2, fields) + plane, jnp.float32),
            ],
            in_specs=[vmem()] * (4 + len(taken)),
        )(pivots, lowers, uppers, scale, *taken)
        other = swap(send, 1, "wall", f"chunk{number}_core")
        chip, inner, outgoing = call(
            functools.partial(pair_kernel, count, chips),
            [vectors, vectors, single],
            micros=0.25 * count,
            scratch=[pltpu.VMEM((2,) + vectors.shape, jnp.float32)],
            in_specs=[vmem()] * 3,
        )(pair, keep, other)
        began.append((source, chip, inner, outgoing))

    if tree:
        upper_half = call(
            upper_half_kernel,
            f32(2, fields, fields, *plane),
            micros=0.7,
            in_specs=[vmem()] * 2,
        )(chip_matrices, beside)
        with jax.named_scope("matrices_inward"):
            upper_half = lax.ppermute(upper_half, "wall", inward)
    for number, chosen in enumerate(CHUNKS):
        count = len(chosen)
        vectors = f32(2, count, 2, fields, *plane)
        single = f32(count, 2, fields, *plane)
        source, chip, inner, outgoing = began[number]
        extra = ()
        if tree:
            with jax.named_scope(f"chunk{number}_to_middle"):
                came = lax.ppermute(outgoing, "wall", outward)
            mine = call(
                functools.partial(halves_kernel, count),
                single,
                micros=0.2 * count,
                in_specs=[vmem()] * 4,
            )(chip_matrices, beside, chip, came)
            with jax.named_scope(f"chunk{number}_middle"):
                across = lax.ppermute(mine, "wall", inward)
            edge, outgoing = call(
                functools.partial(middle_kernel, count),
                [vectors, single],
                micros=0.2 * count,
                in_specs=[vmem()] * 7,
            )(chip_matrices, beside, upper_half, chip, came, mine, across)
            with jax.named_scope(f"chunk{number}_to_ends"):
                extra = (lax.ppermute(outgoing, "wall", outward),)
        else:
            sweep = jnp.zeros(single.shape, jnp.float32)
            answer = jnp.zeros(single.shape, jnp.float32)
            upward = [(i, i + 2) for i in range(walls - 2)]
            downward = [(i + 2, i) for i in range(walls - 2)]
            for _ in range(chips - 1):
                sweep = lax.ppermute(affine(chip_matrices[0], sweep, chip[0]), "wall", upward)
            offset = affine(chip_matrices[2], sweep, chip[1])
            for _ in range(chips - 1):
                answer = lax.ppermute(affine(chip_matrices[1], answer, offset), "wall", downward)
            edge = jnp.stack([sweep, answer])
        keep, send = call(
            functools.partial(split_kernel, count, tree),
            [vectors, vectors],
            micros=0.25 * count,
            scratch=[pltpu.VMEM(vectors.shape, jnp.float32)],
            in_specs=[vmem()] * (4 + len(extra)),
        )(pair, joint, inner, edge, *extra)
        other = swap(send, 1, "wall", f"chunk{number}_apart")
        final = number == len(CHUNKS) - 1
        made = (2, 2, fields, count, half * rows, width)
        scratch = [
            pltpu.VMEM((rows, count, 2, fields) + plane, jnp.float32),
            pltpu.VMEM((2,) + vectors.shape, jnp.float32),
        ]
        if final:
            scratch = [
                pltpu.VMEM(made, jnp.float32),
                pltpu.SemaphoreType.DMA((len(CHUNKS), 2, 2, fields)),
            ] + scratch
        finished.append(
            call(
                functools.partial(answer_kernel, count, chosen[0] if final else None, rows),
                f32(2, fields, columns, *flat) if final else f32(*made),
                micros=1.5 * count,
                scratch=scratch,
                in_specs=[vmem()] * (5 + (len(finished) if final else 0)),
                out_specs=anywhere() if final else vmem(),
            )(lowers, uppers, source, keep, other, *(finished if final else ()))
        )
    out = finished[-1]
    return out.reshape(2, fields, columns, points, rows, width)


def solution(mesh):
    placed = (
        P(None, None, None, "span", "wall", None),
        P(),
        P(None, None, None, "span", "wall", None),
        P(None, None, None, "span", "wall", None),
        P(None, None, None, "span", "wall", None),
    )
    return jax.shard_map(
        local,
        mesh=mesh,
        in_specs=placed,
        out_specs=P(None, None, None, "span", "wall", None),
        check_vma=False,
    )
```
